128 devices in a mesh: space: 8 (over z, y_lo), vel: 16 (over y_hi, x, core).
Axes of the slice: x: 4, y: 4 (y_hi: 2, y_lo: 2; y = y_hi * 2 + y_lo), z: 4, core: 2. Of those that a mesh axis runs over, the one named last changes fastest.
Arguments:
- distribution: bfloat16 [4096, 48, 8, 128], P('vel', 'space'), may hold values from -6 to 6
- up_factor: bfloat16 [4096, 256], P('vel'), may hold values from -0.75 to 0.75
- down_factor: bfloat16 [4096, 256], P('vel'), may hold values from -0.09375 to 0.09375
- decay: float32 [4096], P('vel'), may hold values from 0.3 to 3
- wall_kind: int32 [2, 8, 128], replicated, may hold values from 0 to 2
Outputs:
- advanced: bfloat16 [4096, 48, 8, 128], P('vel', 'space')
The draws below stay inside these ranges and needn't reach their ends.
Inputs may be any that keep to these rules, and one draw needn't show every extreme that they name: `wall_kind`: 0 marks a diffuse wall at rest, 1 a diffuse heated wall, 2 an open face.
All inputs are finite; a program needn't handle non-finite values.
Results may differ from the reference program's by a relative error of at most 0.0046.
Values may be sent and summed in bfloat16 or wider, within the bound.
A program may use at most 192 MiB of HBM per device.

```python
import math
import jax
import jax.numpy as jnp
from jax import lax

NV = 16
R = 256
V = 4096
GX = 8
GY = 128
STEPS = 2
NZ = 48


def place_ends(array, rng, least, top_value):
    longest = array.shape.index(max(array.shape))
    spots = []
    for shift in (0, 1):
        where = [jax.random.randint(jax.random.fold_in(rng, axis), (), 0, length) for axis, length in enumerate(array.shape)]
        where[longest] = (where[longest] + shift) % array.shape[longest]
        spots.append(tuple(where))
    return array.at[spots[0]].set(least).at[spots[1]].set(top_value)


def block_levels(stream_key, dims, cuts, low, high):
    gain = 1.0
    for axis_at, blocks in cuts:
        draws = jax.random.uniform(jax.random.fold_in(jax.random.fold_in(stream_key, 6), axis_at), (blocks,), jnp.float32, low / len(cuts), high / len(cuts))
        gain = gain * jnp.repeat(jnp.exp(draws), dims[axis_at] // blocks).reshape((-1,) + (1,) * (len(dims) - 1 - axis_at))
    return gain


def scatter_about(stream_key, extent, spread, most, pieces=(), kind=jnp.bfloat16):
    level = block_levels(stream_key, extent, pieces, -0.22, 0.18) if pieces else 1.0
    drawn = jax.random.normal(stream_key, extent, jnp.float32) * spread * level
    return jnp.minimum(jnp.maximum(drawn, -most), most).astype(kind)


def setup_inputs(seed: int = 0) -> dict:
    streams_of = jax.random.split(jax.random.key(seed), 6)
    distribution = scatter_about(streams_of[0], (V, NZ, GX, GY), 1.0, 6.0, ((0, 16), (1, 8)))
    up_factor = scatter_about(streams_of[1], (V, R), (R // 4) ** -0.5, 0.75, ((0, 16),))
    down_factor = scatter_about(streams_of[2], (V, R), V ** -0.5, 0.09375, ((0, 16),))
    decay = jnp.clip(jnp.exp(math.log(3.0) - 2.3025851 * jax.random.uniform(streams_of[3], (V,), jnp.float32) ** block_levels(streams_of[3], (V,), ((0, 16),), -0.2, 0.2)), 0.3, 3.0)
    wall_kind = place_ends(jax.random.randint(streams_of[4], (2, GX, GY), 0, 3), jax.random.fold_in(streams_of[4], 1), 0, 2).astype(jnp.int32)
    return {"distribution": distribution, "up_factor": up_factor, "down_factor": down_factor, "decay": decay, "wall_kind": wall_kind}


speed_range = 8.0
time_ratio = 0.08
wall_heat = 3.0


def components(vel_ids):
    spacing = speed_range / NV
    midpoint = (NV - 1) / 2.0
    along_z = ((vel_ids // (NV * NV)).astype(jnp.float32) - midpoint) * spacing
    along_x = (((vel_ids // NV) % NV).astype(jnp.float32) - midpoint) * spacing
    along_y = ((vel_ids % NV).astype(jnp.float32) - midpoint) * spacing
    return along_z, along_x, along_y


def wall_ghost(outflux, kind_face, maxwell, energy, norm):
    sigma = outflux / norm
    heating = jnp.where(kind_face == 1, wall_heat, 0.0)
    opened = jnp.where(kind_face == 2, 0.0, 1.0)
    return maxwell[:, None, None] * (sigma[None] + heating[None] * energy[:, None, None]) * opened[None]


def transport(centre, lower_plane, upper_plane, along_z, along_x, along_y):
    dimensions = centre.ndim
    shaped = (-1,) + (1,) * (dimensions - 1)
    axis_x = dimensions - 2
    axis_y = dimensions - 1
    plus_z = jnp.maximum(along_z, 0.0).reshape(shaped)
    minus_z = jnp.minimum(along_z, 0.0).reshape(shaped)
    plus_x = jnp.maximum(along_x, 0.0).reshape(shaped)
    minus_x = jnp.minimum(along_x, 0.0).reshape(shaped)
    plus_y = jnp.maximum(along_y, 0.0).reshape(shaped)
    minus_y = jnp.minimum(along_y, 0.0).reshape(shaped)
    result = plus_z * (centre - lower_plane) + minus_z * (upper_plane - centre)
    result = result + plus_x * (centre - jnp.roll(centre, 1, axis_x)) + minus_x * (jnp.roll(centre, -1, axis_x) - centre)
    result = result + plus_y * (centre - jnp.roll(centre, 1, axis_y)) + minus_y * (jnp.roll(centre, -1, axis_y) - centre)
    return result


def advance(current, up_factor, down_factor, decay, wall_kind, along_z, along_x, along_y, maxwell, energy, norm):
    depth = current.shape[1]
    low_face = current[:, 0].astype(jnp.float32)
    high_face = current[:, depth - 1].astype(jnp.float32)
    outflux_low = jnp.sum(jnp.maximum(-along_z, 0.0)[:, None, None] * low_face, axis=0)
    outflux_high = jnp.sum(jnp.maximum(along_z, 0.0)[:, None, None] * high_face, axis=0)
    ghost_low = wall_ghost(outflux_low, wall_kind[0], maxwell, energy, norm)
    ghost_high = wall_ghost(outflux_high, wall_kind[1], maxwell, energy, norm)

    def plane(level):
        stored = lax.dynamic_index_in_dim(current, level, 1, keepdims=False)
        centre = stored.astype(jnp.float32)
        lower_raw = lax.dynamic_index_in_dim(current, jnp.maximum(level - 1, 0), 1, keepdims=False)
        upper_raw = lax.dynamic_index_in_dim(current, jnp.minimum(level + 1, depth - 1), 1, keepdims=False)
        lower_plane = jnp.where(level == 0, ghost_low, lower_raw.astype(jnp.float32))
        upper_plane = jnp.where(level == depth - 1, ghost_high, upper_raw.astype(jnp.float32))
        moved = transport(centre, lower_plane, upper_plane, along_z, along_x, along_y)
        flat_rows = stored.reshape(stored.shape[0], -1)
        coeffs = jnp.dot(down_factor.T, flat_rows, preferred_element_type=jnp.float32).astype(jnp.bfloat16)
        gained = jnp.dot(up_factor, coeffs, preferred_element_type=jnp.float32).reshape(centre.shape)
        updated = centre - time_ratio * moved + time_ratio * (gained - decay[:, None, None] * centre)
        return updated.astype(jnp.bfloat16)

    planes = lax.map(plane, jnp.arange(depth, dtype=jnp.int32))
    return jnp.transpose(planes, (1, 0, 2, 3))


def reference(distribution, up_factor, down_factor, decay, wall_kind):
    all_ids = jnp.arange(NV ** 3, dtype=jnp.int32)
    along_z, along_x, along_y = components(all_ids)
    speed_sq = along_z * along_z + along_x * along_x + along_y * along_y
    maxwell = jnp.exp(-0.5 * speed_sq)
    energy = 0.5 * speed_sq - 1.5
    norm = jnp.sum(jnp.maximum(along_z, 0.0) * maxwell)
    current = distribution
    for step in range(STEPS):
        current = advance(current, up_factor, down_factor, decay, wall_kind, along_z, along_x, along_y, maxwell, energy, norm)
    return current
```

```python
import functools

import jax
import jax.numpy as jnp
from jax import lax
from jax.experimental import pallas as pl
from jax.experimental.pallas import tpu as pltpu
from jax.sharding import PartitionSpec as P

NV = 16
STEPS = 2
MESH = pl.DeviceIdType.MESH

speed_range = 8.0
time_ratio = 0.08
wall_heat = 3.0

SPACING = speed_range / NV
MIDPOINT = (NV - 1) / 2.0
F32 = jnp.float32
BF16 = jnp.bfloat16

CORE_SUM, PASS_SUM, NEAR_SUM, LAST_SUM, PAIR_SUM, OUT_B, OUT_A, OUT_PASS, CORE_OUT = range(9)
STAGES = 8


def kernel(
    depth,
    slabs,
    dist_ref,
    up_ref,
    down_ref,
    decay_ref,
    wall_ref,
    out_ref,
    state,
    raw,
    down_t,
    keep,
    slope_x,
    slope_y,
    part,
    sum_core_out,
    sum_core_in,
    sum_a_out,
    sum_a_in,
    sum_b_out,
    sum_b_in,
    sum_y_out,
    sum_y_in,
    coeffs,
    flux_out,
    flux_in,
    send_sem,
    recv_sem,
    halo_send,
    halo_recv,
    flux_send,
    flux_recv,
    in_sem,
    out_sem,
):
    chunks = STEPS * depth
    slab = lax.axis_index("space")
    vel = lax.axis_index("vel")
    core = lax.rem(vel, 2)
    chip = lax.rem(vel // 2, 4)
    upper = vel // 8
    sign = 2 * upper - 1
    flip = chip + 1 - 2 * lax.rem(chip, 2)
    mirror = 3 - chip
    chip_a = flip * (1 - core) + mirror * core
    chip_b = mirror * (1 - core) + flip * core
    chip_o = lax.rem(chip + 2, 4)

    def device(pair, x, c):
        return (slab, pair * 8 + x * 2 + c)

    to_core = device(upper, chip, 1 - core)
    to_a = device(upper, chip_a, core)
    to_b = device(upper, chip_b, core)
    to_pair = device(1 - upper, chip, core)
    to_slab = (slab + sign, vel)
    last = depth - 1
    source_plane = last * upper
    target_plane = last * (1 - upper)
    halo_slot = (depth + 1) * (1 - upper)
    sends_halo = slab != (slabs - 1) * upper
    takes_halo = slab != (slabs - 1) * (1 - upper)

    def level_of(q):
        return lax.rem(depth - lax.rem(q, depth), depth)

    def load(z):
        return pltpu.make_async_copy(dist_ref.at[:, z], raw.at[z], in_sem.at[z])

    def store(z):
        return pltpu.make_async_copy(raw.at[z], out_ref.at[:, z], out_sem.at[z])

    def remote(kind, q, src, dst, target):
        return pltpu.make_async_remote_copy(
            src_ref=src,
            dst_ref=dst,
            send_sem=send_sem.at[kind, q],
            recv_sem=recv_sem.at[kind, q],
            device_id=target,
            device_id_type=MESH,
        )

    mine = core * 4

    def message(kind, q):
        if kind == CORE_SUM:
            return remote(kind, q, sum_core_out.at[q], sum_core_in.at[q], to_core)
        if kind == PASS_SUM:
            return remote(kind, q, sum_a_out.at[q, 0], sum_a_in.at[q, 0], to_a)
        if kind == NEAR_SUM:
            return remote(kind, q, sum_a_out.at[q, 1], sum_a_in.at[q, 1], to_a)
        if kind == LAST_SUM:
            return remote(kind, q, sum_b_out.at[q], sum_b_in.at[q], to_b)
        if kind == PAIR_SUM:
            return remote(kind, q, sum_y_out.at[q], sum_y_in.at[q], to_pair)
        if kind == OUT_B:
            row = coeffs.at[q, mine + chip]
            return remote(kind, q, row, row, to_b)
        if kind == OUT_A:
            row = coeffs.at[q, mine + chip]
            return remote(kind, q, row, row, to_a)
        if kind == OUT_PASS:
            row = coeffs.at[q, mine + chip_b]
            return remote(kind, q, row, row, to_a)
        rows = coeffs.at[q, pl.ds(mine, 4)]
        return remote(kind, q, rows, rows, to_core)

    def halo(n):
        return pltpu.make_async_remote_copy(
            src_ref=state.at[n, 1 + source_plane],
            dst_ref=state.at[n, halo_slot],
            send_sem=halo_send.at[n],
            recv_sem=halo_recv.at[n],
            device_id=to_slab,
            device_id_type=MESH,
        )

    def flux(n, k):
        return pltpu.make_async_remote_copy(
            src_ref=flux_out.at[n],
            dst_ref=flux_in.at[n, chip * 2 + core],
            send_sem=flux_send.at[n, k],
            recv_sem=flux_recv.at[n, chip * 2 + core],
            device_id=(slab, (1 - upper) * 8 + k),
            device_id_type=MESH,
        )

    def flux_arrival(n, k):
        return pltpu.make_async_remote_copy(
            src_ref=flux_out.at[n],
            dst_ref=flux_in.at[n, k],
            send_sem=flux_send.at[n, k],
            recv_sem=flux_recv.at[n, k],
            device_id=(slab, (1 - upper) * 8 + k),
            device_id_type=MESH,
        )

    for z in range(depth):
        load((depth - z) % depth).start()

    barrier = pltpu.get_barrier_semaphore()

    def greet(target):
        pl.semaphore_signal(barrier, inc=1, device_id=target, device_id_type=MESH)

    for target in (to_core, to_a, to_b):
        greet(target)
    for k in range(8):
        greet((slab, (1 - upper) * 8 + k))

    greet((lax.rem(slab + slabs - 1, slabs), vel))
    greet((lax.rem(slab + 1, slabs), vel))

    ids = lax.broadcasted_iota(jnp.int32, (256, 128), 0)
    speed_x = jnp.abs(((ids >> 4).astype(F32) - MIDPOINT) * SPACING)
    speed_y = jnp.abs(((ids & 15).astype(F32) - MIDPOINT) * SPACING)
    speed_z = jnp.abs((vel.astype(F32) - MIDPOINT) * SPACING)
    decay = jnp.concatenate(
        [jnp.broadcast_to(decay_ref[i : i + 1, :], (128, 128)).T for i in range(2)], axis=0
    )
    keep[...] = 1.0 - time_ratio * (speed_x + speed_y + speed_z + decay)
    slope_x[...] = time_ratio * speed_x
    slope_y[...] = time_ratio * speed_y
    slope_z = time_ratio * speed_z
    down_t[...] = down_ref[...].T

    pl.semaphore_wait(barrier, 13)

    def project(n, z, x):
        pair = jnp.concatenate([state[n, 1 + z, x], state[n, 1 + z, x + 1]], axis=1)
        return jnp.dot(down_t[...], pair, preferred_element_type=F32)

    def begin(q):
        n, z = q // depth, level_of(q)

        @pl.when(q < depth)
        def _():
            load(z).wait()

            def block(i, carry):
                rows = pl.ds(pl.multiple_of(i * 16, 16), 16)
                state[0, 1 + z, :, rows, :] = jnp.swapaxes(raw[z, rows], 0, 1)
                return carry

            lax.fori_loop(0, 16, block, 0)

        @pl.when(z == source_plane)
        def _():
            @pl.when(sends_halo)
            def _():
                halo(n).start()

            @pl.when(jnp.logical_not(sends_halo))
            def _():
                for x in range(8):
                    plane = state[n, 1 + z, x].astype(F32)
                    flux_out[n, x : x + 1, :] = speed_z * jnp.sum(plane, axis=0, keepdims=True)
                for k in range(8):
                    flux(n, k).start()

        for j in range(2):
            both = project(n, z, (1 - core) * 4 + 2 * j)
            sum_core_out[q, 2 * j] = both[:, :128].astype(BF16)
            sum_core_out[q, 2 * j + 1] = both[:, 128:].astype(BF16)
        message(CORE_SUM, q).start()
        for j in range(2):
            both = project(n, z, mine + 2 * j)
            part[q, 2 * j] = both[:, :128]
            part[q, 2 * j + 1] = both[:, 128:]

    def chip_sum(q, j):
        return part[q, j] + sum_core_in[q, j].astype(F32)

    def first_sums(q):
        message(CORE_SUM, q).wait_recv()
        sum_a_out[q, 0] = chip_sum(q, chip_o).astype(BF16)
        message(PASS_SUM, q).start()
        sum_a_out[q, 1] = chip_sum(q, chip_a).astype(BF16)
        message(NEAR_SUM, q).start()

    def second_sums(q):
        message(PASS_SUM, q).wait_recv()
        sum_b_out[q] = (chip_sum(q, chip_b) + sum_a_in[q, 0].astype(F32)).astype(BF16)
        message(LAST_SUM, q).start()

    def third_sums(q):
        message(NEAR_SUM, q).wait_recv()
        message(LAST_SUM, q).wait_recv()
        total = chip_sum(q, chip) + sum_a_in[q, 1].astype(F32) + sum_b_in[q].astype(F32)
        part[q, chip] = total
        sum_y_out[q] = total.astype(BF16)
        message(PAIR_SUM, q).start()

    def finish_sums(q):
        message(PAIR_SUM, q).wait_recv()
        coeffs[q, mine + chip] = (part[q, chip] + sum_y_in[q].astype(F32)).astype(BF16)
        message(OUT_B, q).start()
        message(OUT_A, q).start()

    def pass_on(q):
        message(OUT_B, q).wait_recv()
        message(OUT_PASS, q).start()

    def cross(q):
        message(OUT_A, q).wait_recv()
        message(OUT_PASS, q).wait_recv()
        message(CORE_OUT, q).start()

    def wall(n):
        for k in range(8):
            flux_arrival(n, k).wait_recv()
        line = (lax.broadcasted_iota(jnp.int32, (8, 128), 1).astype(F32) - MIDPOINT) * SPACING
        valid = lax.broadcasted_iota(jnp.int32, (8, 128), 1) < NV
        gauss = jnp.where(valid, jnp.exp(-0.5 * line * line), 0.0)
        flow = jnp.sum(jnp.maximum(line, 0.0) * gauss, axis=1, keepdims=True)
        mass = jnp.sum(gauss, axis=1, keepdims=True)
        norm = flow * mass * mass
        out = flux_in[n, 0]
        for k in range(1, 8):
            out = out + flux_in[n, k]
        kind = wall_ref[1 - upper]
        opened = jnp.where(kind == 2, 0.0, 1.0)
        sigma = out / norm * opened
        heating = jnp.where(kind == 1, wall_heat, 0.0)
        rows = lax.broadcasted_iota(jnp.int32, (256, 128), 0)
        one_x = ((rows >> 4).astype(F32) - MIDPOINT) * SPACING
        one_y = ((rows & 15).astype(F32) - MIDPOINT) * SPACING
        half_sq = 0.5 * (one_x * one_x + one_y * one_y + speed_z * speed_z)
        maxwell = jnp.exp(-half_sq)
        energy = half_sq - 1.5
        for x in range(8):
            ghost = maxwell * (sigma[x : x + 1] + heating[x : x + 1] * energy)
            state[n, halo_slot, x] = ghost.astype(BF16)

    def update(q):
        n, z = q // depth, level_of(q)
        message(CORE_OUT, q).wait_recv()

        @pl.when(z == target_plane)
        def _():
            @pl.when(takes_halo)
            def _():
                halo(n).wait_recv()

            @pl.when(jnp.logical_not(takes_halo))
            def _():
                wall(n)

        def row_pair(i, carry):
            pair = jnp.concatenate([coeffs[q, 2 * i], coeffs[q, 2 * i + 1]], axis=1)
            gained = jnp.dot(up_ref[...], pair, preferred_element_type=F32)
            for side in range(2):
                x = 2 * i + side
                for half in range(2):
                    rows = slice(128 * half, 128 * half + 128)
                    beside = lax.rem(x + (1 if half == 0 else 7), 8)
                    centre = state[n, 1 + z, x, rows].astype(F32)
                    wind_z = state[n, 1 + z - sign, x, rows].astype(F32)
                    wind_x = state[n, 1 + z, beside, rows].astype(F32)
                    split = centre.reshape(8, 16, 128)
                    wind_y = jnp.concatenate(
                        [pltpu.roll(split[:, :8], 127, 2), pltpu.roll(split[:, 8:], 1, 2)], axis=1
                    ).reshape(128, 128)
                    new = (
                        keep[rows] * centre
                        + slope_z * wind_z
                        + slope_x[rows] * wind_x
                        + slope_y[rows] * wind_y
                        + time_ratio * gained[rows, 128 * side : 128 * side + 128]
                    )
                    state[n + 1, 1 + z, x, rows] = new.astype(BF16)
            return carry

        lax.fori_loop(0, 4, row_pair, 0)

        @pl.when(q >= depth)
        def _():
            def block(i, carry):
                rows = pl.ds(pl.multiple_of(i * 16, 16), 16)
                raw[z, rows] = jnp.swapaxes(state[STEPS, 1 + z, :, rows, :], 0, 1)
                return carry

            lax.fori_loop(0, 16, block, 0)
            store(z).start()

    order = [
        (cross, 6),
        (pass_on, 5),
        (finish_sums, 4),
        (third_sums, 3),
        (second_sums, 2),
        (first_sums, 1),
        (update, 7),
        (begin, 0),
    ]

    def tick(t, carry):
        for act, lag in order:
            entry = t - lag
            q = entry - entry // (depth + 1)

            @pl.when((entry >= 0) & (entry <= chunks) & (entry != depth))
            def _(act=act, q=q):
                act(q)

        return carry

    lax.fori_loop(0, chunks + STAGES, tick, 0)

    def drain(q, carry):
        for kind in range(9):
            message(kind, q).wait_send()
        return carry

    lax.fori_loop(0, chunks, drain, 0)

    @pl.when(sends_halo)
    def _():
        for n in range(STEPS):
            halo(n).wait_send()

    @pl.when(jnp.logical_not(sends_halo))
    def _():
        for n in range(STEPS):
            for k in range(8):
                flux(n, k).wait_send()

    for z in range(depth):
        store(z).wait()


def body(slabs, distribution, up_factor, down_factor, decay, wall_kind):
    local_vel, depth, width_x, width_y = distribution.shape
    rank = up_factor.shape[1]
    chunks = STEPS * depth
    piece = (rank, width_y)
    vmem = pl.BlockSpec(memory_space=pltpu.VMEM)
    anywhere = pl.BlockSpec(memory_space=pl.ANY)
    dma = pltpu.SemaphoreType.DMA
    return pl.pallas_call(
        functools.partial(kernel, depth, slabs),
        out_shape=jax.ShapeDtypeStruct(distribution.shape, distribution.dtype),
        in_specs=[anywhere, vmem, vmem, vmem, vmem],
        out_specs=anywhere,
        scratch_shapes=[
            pltpu.VMEM((STEPS + 1, depth + 2, width_x, local_vel, width_y), BF16),
            pltpu.VMEM((depth, local_vel, width_x, width_y), BF16),
            pltpu.VMEM((rank, local_vel), BF16),
            pltpu.VMEM((local_vel, width_y), F32),
            pltpu.VMEM((local_vel, width_y), F32),
            pltpu.VMEM((local_vel, width_y), F32),
            pltpu.VMEM((chunks, 4) + piece, F32),
            pltpu.VMEM((chunks, 4) + piece, BF16),
            pltpu.VMEM((chunks, 4) + piece, BF16),
            pltpu.VMEM((chunks, 2) + piece, BF16),
            pltpu.VMEM((chunks, 2) + piece, BF16),
            pltpu.VMEM((chunks,) + piece, BF16),
            pltpu.VMEM((chunks,) + piece, BF16),
            pltpu.VMEM((chunks,) + piece, BF16),
            pltpu.VMEM((chunks,) + piece, BF16),
            pltpu.VMEM((chunks, 8) + piece, BF16),
            pltpu.VMEM((STEPS, width_x, width_y), F32),
            pltpu.VMEM((STEPS, 8, width_x, width_y), F32),
            dma((9, chunks)),
            dma((9, chunks)),
            dma((STEPS,)),
            dma((STEPS,)),
            dma((STEPS, 8)),
            dma((STEPS, 8)),
            dma((depth,)),
            dma((depth,)),
        ],
        compiler_params=pltpu.CompilerParams(
            collective_id=0, has_side_effects=True, vmem_limit_bytes=56 * 2**20
        ),
        cost_estimate=pl.CostEstimate(
            flops=4 * STEPS * local_vel * rank * depth * width_x * width_y,
            bytes_accessed=4 * distribution.size,
            transcendentals=0,
        ),
        name="boltzmann_steps",
    )(distribution, up_factor, down_factor, decay.reshape(2, -1), wall_kind)


def solution(mesh):
    return jax.shard_map(
        functools.partial(body, mesh.shape["space"]),
        mesh=mesh,
        in_specs=(P("vel", "space", None, None), P("vel", None), P("vel", None), P("vel"), P()),
        out_specs=P("vel", "space", None, None),
        check_vma=False,
    )
```

```python
import functools
from typing import Any, NamedTuple

import jax
import jax.numpy as jnp
from jax import lax
from jax.experimental import pallas as pl
from jax.experimental.pallas import tpu as pltpu
from jax.sharding import PartitionSpec as P

NV = 16
STEPS = 2
MESH = pl.DeviceIdType.MESH
VMEM_MIB = 56

speed_range = 8.0
time_ratio = 0.08
wall_heat = 3.0

SPACING = speed_range / NV
MIDPOINT = (NV - 1) / 2.0
F32 = jnp.float32
BF16 = jnp.bfloat16

CORE_SUM, PASS_SUM, NEAR_SUM, LAST_SUM, PAIR_SUM, OUT_B, OUT_A, OUT_PASS, CORE_OUT = range(9)
LAG_BEGIN, LAG_FIRST, LAG_SECOND, LAG_THIRD, LAG_FINISH, LAG_PASS, LAG_CROSS, LAG_UPDATE = (
    0, 1, 3, 5, 7, 9, 11, 12,
)
EDGE_TICK = 7


class Lane(NamedTuple):
    part: Any
    core_out: Any
    core_in: Any
    a_out: Any
    a_in: Any
    b_out: Any
    b_in: Any
    y_out: Any
    y_in: Any
    coeffs: Any
    send: Any
    recv: Any


def kernel(
    depth,
    slabs,
    dist_ref,
    up_ref,
    down_ref,
    decay_ref,
    wall_ref,
    out_ref,
    state,
    raw,
    down_t,
    mix,
    keep,
    slope_x,
    slope_y,
    flux_out,
    flux_in,
    halo_send,
    halo_recv,
    flux_send,
    flux_recv,
    in_sem,
    out_sem,
    *lane_refs,
):
    count = len(Lane._fields)
    cells = Lane(*lane_refs[:count])
    extra = Lane(*lane_refs[count:])
    chunks = STEPS * depth
    slab = lax.axis_index("space")
    vel = lax.axis_index("vel")
    core = lax.rem(vel, 2)
    chip = lax.rem(vel // 2, 4)
    upper = vel // 8
    sign = 2 * upper - 1
    flip = chip + 1 - 2 * lax.rem(chip, 2)
    mirror = 3 - chip
    chip_a = flip * (1 - core) + mirror * core
    chip_b = mirror * (1 - core) + flip * core
    chip_o = lax.rem(chip + 2, 4)

    def device(pair, x, c):
        return (slab, pair * 8 + x * 2 + c)

    to_core = device(upper, chip, 1 - core)
    to_a = device(upper, chip_a, core)
    to_b = device(upper, chip_b, core)
    to_pair = device(1 - upper, chip, core)
    to_slab = (lax.rem(slab + sign + slabs, slabs), vel)
    last = depth - 1
    source_plane = last * upper
    target_plane = last * (1 - upper)
    halo_slot = (depth + 1) * (1 - upper)
    sends_halo = slab != (slabs - 1) * upper
    takes_halo = slab != (slabs - 1) * (1 - upper)
    mine = core * 4
    theirs = 4 - mine

    def level_of(q):
        return lax.rem(2 * depth - q + (depth - 2) * (q // depth), depth)

    def load(z):
        return pltpu.make_async_copy(dist_ref.at[:, z], raw.at[z], in_sem.at[z])

    def store(z):
        return pltpu.make_async_copy(raw.at[z], out_ref.at[:, z], out_sem.at[z])

    def message(kind, lane, q):
        own = lane.coeffs.at[q, mine + chip]
        if kind == CORE_SUM:
            src, dst, target = lane.core_out.at[q], lane.core_in.at[q], to_core
        elif kind == PASS_SUM:
            src, dst, target = lane.a_out.at[q, 0], lane.a_in.at[q, 0], to_a
        elif kind == NEAR_SUM:
            src, dst, target = lane.a_out.at[q, 1], lane.a_in.at[q, 1], to_a
        elif kind == LAST_SUM:
            src, dst, target = lane.b_out.at[q], lane.b_in.at[q], to_b
        elif kind == PAIR_SUM:
            src, dst, target = lane.y_out.at[q], lane.y_in.at[q], to_pair
        elif kind == OUT_B:
            src, dst, target = own, own, to_b
        elif kind == OUT_A:
            src, dst, target = own, own, to_a
        elif kind == OUT_PASS:
            src = lane.coeffs.at[q, mine + chip_b]
            dst, target = src, to_a
        else:
            src = lane.coeffs.at[q, pl.ds(mine, 4)]
            dst, target = src, to_core
        return pltpu.make_async_remote_copy(
            src_ref=src,
            dst_ref=dst,
            send_sem=lane.send.at[kind, q],
            recv_sem=lane.recv.at[kind, q],
            device_id=target,
            device_id_type=MESH,
        )

    def halo(n):
        return pltpu.make_async_remote_copy(
            src_ref=state.at[n, 1 + source_plane],
            dst_ref=state.at[n, halo_slot],
            send_sem=halo_send.at[n],
            recv_sem=halo_recv.at[n],
            device_id=to_slab,
            device_id_type=MESH,
        )

    def flux(n, k, sender):
        return pltpu.make_async_remote_copy(
            src_ref=flux_out.at[n],
            dst_ref=flux_in.at[n, sender],
            send_sem=flux_send.at[n, k],
            recv_sem=flux_recv.at[n, sender],
            device_id=(slab, (1 - upper) * 8 + k),
            device_id_type=MESH,
        )

    for q in range(depth):
        load((depth - q) % depth).start()

    barrier = pltpu.get_barrier_semaphore()

    def greet(target):
        pl.semaphore_signal(barrier, inc=1, device_id=target, device_id_type=MESH)

    for target in (to_core, to_a, to_b):
        greet(target)
    for k in range(8):
        greet((slab, (1 - upper) * 8 + k))
    greet((lax.rem(slab + slabs - 1, slabs), vel))
    greet((lax.rem(slab + 1, slabs), vel))

    down_t[...] = down_ref[...].T
    for j in range(4):
        for base, left in ((theirs, True), (mine, False)):
            rows = pl.ds(pl.multiple_of((base + j) * 32, 32), 32)
            both = jnp.dot(down_t[rows, :], up_ref[...], preferred_element_type=F32)
            for side in range(2):
                value = both[:, 128 * side : 128 * side + 128]
                if left:
                    extra.core_out[0, j, 32 * side : 32 * side + 32] = value.astype(BF16)
                else:
                    extra.part[0, j, 32 * side : 32 * side + 32] = value
    ids = lax.broadcasted_iota(jnp.int32, (256, 128), 0)
    speed_x = jnp.abs(((ids >> 4).astype(F32) - MIDPOINT) * SPACING)
    speed_y = jnp.abs(((ids & 15).astype(F32) - MIDPOINT) * SPACING)
    speed_z = jnp.abs((vel.astype(F32) - MIDPOINT) * SPACING)
    decay = jnp.concatenate(
        [jnp.broadcast_to(decay_ref[i : i + 1, :], (128, 128)).T for i in range(2)], axis=0
    )
    keep[...] = 1.0 - time_ratio * (speed_x + speed_y + speed_z + decay)
    slope_x[...] = time_ratio * speed_x
    slope_y[...] = time_ratio * speed_y
    slope_z = time_ratio * speed_z

    def arrange(q, carry):
        z = level_of(q)
        load(z).wait()

        def block(i, inner):
            rows = pl.ds(pl.multiple_of(i * 16, 16), 16)
            state[0, 1 + z, :, rows, :] = jnp.swapaxes(raw[z, rows], 0, 1)
            return inner

        return lax.fori_loop(0, 16, block, carry)

    lax.fori_loop(0, depth, arrange, 0)
    pl.semaphore_wait(barrier, 13)

    def send_edge(n):
        @pl.when(sends_halo)
        def _():
            halo(n).start()

        @pl.when(jnp.logical_not(sends_halo))
        def _():
            for x in range(8):
                plane = state[n, 1 + source_plane, x].astype(F32)
                flux_out[n, x : x + 1, :] = speed_z * jnp.sum(plane, axis=0, keepdims=True)
            for k in range(8):
                flux(n, k, chip * 2 + core).start()

    def take_edge(n):
        @pl.when(takes_halo)
        def _():
            halo(n).wait_recv()

        @pl.when(jnp.logical_not(takes_halo))
        def _():
            wall(n)

    def wall(n):
        for k in range(8):
            flux(n, k, k).wait_recv()
        line = (lax.broadcasted_iota(jnp.int32, (8, 128), 1).astype(F32) - MIDPOINT) * SPACING
        valid = lax.broadcasted_iota(jnp.int32, (8, 128), 1) < NV
        gauss = jnp.where(valid, jnp.exp(-0.5 * line * line), 0.0)
        flow = jnp.sum(jnp.maximum(line, 0.0) * gauss, axis=1, keepdims=True)
        mass = jnp.sum(gauss, axis=1, keepdims=True)
        norm = flow * mass * mass
        out = flux_in[n, 0]
        for k in range(1, 8):
            out = out + flux_in[n, k]
        kind = wall_ref[1 - upper]
        opened = jnp.where(kind == 2, 0.0, 1.0)
        sigma = out / norm * opened
        heating = jnp.where(kind == 1, wall_heat, 0.0)
        rows = lax.broadcasted_iota(jnp.int32, (256, 128), 0)
        one_x = ((rows >> 4).astype(F32) - MIDPOINT) * SPACING
        one_y = ((rows & 15).astype(F32) - MIDPOINT) * SPACING
        half_sq = 0.5 * (one_x * one_x + one_y * one_y + speed_z * speed_z)
        maxwell = jnp.exp(-half_sq)
        energy = half_sq - 1.5
        for x in range(8):
            ghost = maxwell * (sigma[x : x + 1] + heating[x : x + 1] * energy)
            state[n, halo_slot, x] = ghost.astype(BF16)

    def drift(n, z, x, half):
        rows = slice(128 * half, 128 * half + 128)
        beside = lax.rem(x + (1 if half == 0 else 7), 8)
        centre = state[n, 1 + z, x, rows].astype(F32)
        wind_z = state[n, 1 + z - sign, x, rows].astype(F32)
        wind_x = state[n, 1 + z, beside, rows].astype(F32)
        split = centre.reshape(8, 16, 128)
        wind_y = jnp.concatenate(
            [pltpu.roll(split[:, :8], 127, 2), pltpu.roll(split[:, 8:], 1, 2)], axis=1
        ).reshape(128, 128)
        return (
            keep[rows] * centre
            + slope_z * wind_z
            + slope_x[rows] * wind_x
            + slope_y[rows] * wind_y
        )

    def begin(q):
        n, z = q // depth, level_of(q)

        @pl.when(q >= depth)
        def _():
            def row(x, carry):
                for half in range(2):
                    rows = slice(128 * half, 128 * half + 128)
                    state[STEPS, 1 + z, x, rows] = drift(0, z, x, half).astype(BF16)
                return carry

            lax.fori_loop(0, 8, row, 0)

        def project(x):
            pair = jnp.concatenate(
                [state[STEPS * n, 1 + z, x], state[STEPS * n, 1 + z, x + 1]], axis=1
            )
            return jnp.dot(down_t[...], pair, preferred_element_type=F32)

        for j in range(2):
            both = project(theirs + 2 * j)
            cells.core_out[q, 2 * j] = both[:, :128].astype(BF16)
            cells.core_out[q, 2 * j + 1] = both[:, 128:].astype(BF16)
        message(CORE_SUM, cells, q).start()
        for j in range(2):
            both = project(mine + 2 * j)
            cells.part[q, 2 * j] = both[:, :128]
            cells.part[q, 2 * j + 1] = both[:, 128:]

    def chip_sum(lane, q, j):
        return lane.part[q, j] + lane.core_in[q, j].astype(F32)

    def first_sums(lane, q):
        message(CORE_SUM, lane, q).wait_recv()
        lane.a_out[q, 0] = chip_sum(lane, q, chip_o).astype(BF16)
        message(PASS_SUM, lane, q).start()
        lane.a_out[q, 1] = chip_sum(lane, q, chip_a).astype(BF16)
        message(NEAR_SUM, lane, q).start()

    def second_sums(lane, q):
        message(PASS_SUM, lane, q).wait_recv()
        total = chip_sum(lane, q, chip_b) + lane.a_in[q, 0].astype(F32)
        lane.b_out[q] = total.astype(BF16)
        message(LAST_SUM, lane, q).start()

    def third_sums(lane, q):
        message(NEAR_SUM, lane, q).wait_recv()
        message(LAST_SUM, lane, q).wait_recv()
        total = chip_sum(lane, q, chip) + lane.a_in[q, 1].astype(F32)
        total = total + lane.b_in[q].astype(F32)
        lane.part[q, chip] = total
        lane.y_out[q] = total.astype(BF16)
        message(PAIR_SUM, lane, q).start()

    def finish_sums(lane, q):
        message(PAIR_SUM, lane, q).wait_recv()
        if lane is cells:

            @pl.when(q >= depth)
            def _():
                before = lax.rem(depth - level_of(q), depth)
                known = lane.coeffs[before, mine + chip]
                gain = jnp.dot(mix[...], known, preferred_element_type=F32)
                lane.part[q, chip] += time_ratio * gain

        total = lane.part[q, chip] + lane.y_in[q].astype(F32)
        lane.coeffs[q, mine + chip] = total.astype(BF16)
        message(OUT_B, lane, q).start()
        message(OUT_A, lane, q).start()

    def pass_on(lane, q):
        message(OUT_B, lane, q).wait_recv()
        message(OUT_PASS, lane, q).start()

    def cross(lane, q):
        message(OUT_A, lane, q).wait_recv()
        message(OUT_PASS, lane, q).wait_recv()
        message(CORE_OUT, lane, q).start()

    def finish_mix():
        message(CORE_OUT, extra, 0).wait_recv()
        for j in range(8):
            for side in range(2):
                piece = extra.coeffs[0, j, 32 * side : 32 * side + 32]
                mix[32 * j : 32 * j + 32, 128 * side : 128 * side + 128] = piece

    def update(q):
        n, z = q // depth, level_of(q)
        message(CORE_OUT, cells, q).wait_recv()

        @pl.when((q >= depth) & (z == target_plane))
        def _():
            take_edge(1)

        def row_pair(i, carry):
            pair = jnp.concatenate([cells.coeffs[q, 2 * i], cells.coeffs[q, 2 * i + 1]], axis=1)
            gained = jnp.dot(up_ref[...], pair, preferred_element_type=F32)
            for side in range(2):
                x = 2 * i + side
                for half in range(2):
                    rows = slice(128 * half, 128 * half + 128)
                    new = (
                        drift(n, z, x, half)
                        + time_ratio * gained[rows, 128 * side : 128 * side + 128]
                    )
                    state[n + 1, 1 + z, x, rows] = new.astype(BF16)
            return carry

        lax.fori_loop(0, 4, row_pair, 0)

        @pl.when((q < depth) & (z == source_plane))
        def _():
            send_edge(1)

        @pl.when(q >= depth)
        def _():
            def block(i, carry):
                rows = pl.ds(pl.multiple_of(i * 16, 16), 16)
                raw[z, rows] = jnp.swapaxes(state[STEPS, 1 + z, :, rows, :], 0, 1)
                return carry

            lax.fori_loop(0, 16, block, 0)
            store(z).start()

    order = [
        (cross, LAG_CROSS),
        (pass_on, LAG_PASS),
        (finish_sums, LAG_FINISH),
        (third_sums, LAG_THIRD),
        (second_sums, LAG_SECOND),
        (first_sums, LAG_FIRST),
    ]

    def tick(t, carry):
        @pl.when(t == LAG_UPDATE)
        def _():
            finish_mix()

        for act, lag in order:

            @pl.when(t == lag)
            def _(act=act):
                act(extra, 0)

            @pl.when((t >= lag) & (t < lag + chunks))
            def _(act=act, lag=lag):
                act(cells, t - lag)

        @pl.when(t == EDGE_TICK)
        def _():
            take_edge(0)

        @pl.when(t >= LAG_UPDATE)
        def _():
            update(t - LAG_UPDATE)

        @pl.when(t < chunks)
        def _():
            begin(t)

        return carry

    message(CORE_SUM, extra, 0).start()
    send_edge(0)
    lax.fori_loop(0, chunks + LAG_UPDATE, tick, 0)

    def drain(q, carry):
        for kind in range(9):
            message(kind, cells, q).wait_send()
        return carry

    lax.fori_loop(0, chunks, drain, 0)
    for kind in range(9):
        message(kind, extra, 0).wait_send()

    @pl.when(sends_halo)
    def _():
        for n in range(STEPS):
            halo(n).wait_send()

    @pl.when(jnp.logical_not(sends_halo))
    def _():
        for n in range(STEPS):
            for k in range(8):
                flux(n, k, chip * 2 + core).wait_send()

    for z in range(depth):
        store(z).wait()


def lane_shapes(chunks, piece):
    def vmem(lead, kind):
        return pltpu.VMEM((chunks,) + lead + piece, kind)

    return Lane(
        part=vmem((4,), F32),
        core_out=vmem((4,), BF16),
        core_in=vmem((4,), BF16),
        a_out=vmem((2,), BF16),
        a_in=vmem((2,), BF16),
        b_out=vmem((), BF16),
        b_in=vmem((), BF16),
        y_out=vmem((), BF16),
        y_in=vmem((), BF16),
        coeffs=vmem((8,), BF16),
        send=pltpu.SemaphoreType.DMA((9, chunks)),
        recv=pltpu.SemaphoreType.DMA((9, chunks)),
    )


def body(slabs, distribution, up_factor, down_factor, decay, wall_kind):
    local_vel, depth, width_x, width_y = distribution.shape
    rank = up_factor.shape[1]
    vmem = pl.BlockSpec(memory_space=pltpu.VMEM)
    anywhere = pl.BlockSpec(memory_space=pl.ANY)
    dma = pltpu.SemaphoreType.DMA
    return pl.pallas_call(
        functools.partial(kernel, depth, slabs),
        out_shape=jax.ShapeDtypeStruct(distribution.shape, distribution.dtype),
        in_specs=[anywhere, vmem, vmem, vmem, vmem],
        out_specs=anywhere,
        scratch_shapes=[
            pltpu.VMEM((STEPS + 1, depth + 2, width_x, local_vel, width_y), BF16),
            pltpu.VMEM((depth, local_vel, width_x, width_y), BF16),
            pltpu.VMEM((rank, local_vel), BF16),
            pltpu.VMEM((rank, rank), BF16),
            pltpu.VMEM((local_vel, width_y), F32),
            pltpu.VMEM((local_vel, width_y), F32),
            pltpu.VMEM((local_vel, width_y), F32),
            pltpu.VMEM((STEPS, width_x, width_y), F32),
            pltpu.VMEM((STEPS, 8, width_x, width_y), F32),
            dma((STEPS,)),
            dma((STEPS,)),
            dma((STEPS, 8)),
            dma((STEPS, 8)),
            dma((depth,)),
            dma((depth,)),
            *lane_shapes(STEPS * depth, (rank, width_y)),
            *lane_shapes(1, (rank // 4, width_y)),
        ],
        compiler_params=pltpu.CompilerParams(
            collective_id=0, has_side_effects=True, vmem_limit_bytes=VMEM_MIB * 2**20
        ),
        cost_estimate=pl.CostEstimate(
            flops=4 * STEPS * local_vel * rank * depth * width_x * width_y,
            bytes_accessed=4 * distribution.size,
            transcendentals=0,
        ),
        name="boltzmann_steps",
    )(distribution, up_factor, down_factor, decay.reshape(2, -1), wall_kind)


def solution(mesh):
    return jax.shard_map(
        functools.partial(body, mesh.shape["space"]),
        mesh=mesh,
        in_specs=(P("vel", "space", None, None), P("vel", None), P("vel", None), P("vel"), P()),
        out_specs=P("vel", "space", None, None),
        check_vma=False,
    )
```

```python
import functools
from typing import Any, NamedTuple

import jax
import jax.numpy as jnp
from jax import lax
from jax.experimental import pallas as pl
from jax.experimental.pallas import tpu as pltpu
from jax.sharding import PartitionSpec as P

NV = 16
STEPS = 2
MESH = pl.DeviceIdType.MESH
VMEM_MIB = 56

speed_range = 8.0
time_ratio = 0.08
wall_heat = 3.0

SPACING = speed_range / NV
MIDPOINT = (NV - 1) / 2.0
F32 = jnp.float32
BF16 = jnp.bfloat16

CORE_SUM, PASS_SUM, NEAR_SUM, LAST_SUM, PAIR_SUM, OUT_B, OUT_A, OUT_PASS, CORE_OUT = range(9)
LAG_BEGIN, LAG_FIRST, LAG_SECOND, LAG_THIRD, LAG_FINISH, LAG_PASS, LAG_CROSS, LAG_UPDATE = (
    0, 1, 3, 5, 7, 9, 11, 12,
)
EDGE_TICK = 10


class Lane(NamedTuple):
    part: Any
    core_out: Any
    core_in: Any
    a_out: Any
    a_in: Any
    b_out: Any
    b_in: Any
    y_out: Any
    y_in: Any
    coeffs: Any
    send: Any
    recv: Any


def kernel(
    depth,
    slabs,
    dist_ref,
    up_ref,
    down_ref,
    decay_ref,
    wall_ref,
    out_ref,
    state,
    raw,
    down_t,
    mix,
    keep,
    slope_x,
    slope_y,
    flux_out,
    flux_in,
    halo_send,
    halo_recv,
    flux_send,
    flux_recv,
    in_sem,
    *lane_refs,
):
    count = len(Lane._fields)
    cells = Lane(*lane_refs[:count])
    extra = Lane(*lane_refs[count:])
    chunks = STEPS * depth
    slab = lax.axis_index("space")
    vel = lax.axis_index("vel")
    core = lax.rem(vel, 2)
    chip = lax.rem(vel // 2, 4)
    upper = vel // 8
    sign = 2 * upper - 1
    flip = chip + 1 - 2 * lax.rem(chip, 2)
    mirror = 3 - chip
    chip_a = flip * (1 - core) + mirror * core
    chip_b = mirror * (1 - core) + flip * core
    chip_o = lax.rem(chip + 2, 4)

    def device(pair, x, c):
        return (slab, pair * 8 + x * 2 + c)

    to_core = device(upper, chip, 1 - core)
    to_a = device(upper, chip_a, core)
    to_b = device(upper, chip_b, core)
    to_pair = device(1 - upper, chip, core)
    to_slab = (lax.rem(slab + sign + slabs, slabs), vel)
    last = depth - 1
    source_plane = last * upper
    target_plane = last * (1 - upper)
    halo_slot = (depth + 1) * (1 - upper)
    sends_halo = slab != (slabs - 1) * upper
    takes_halo = slab != (slabs - 1) * (1 - upper)
    mine = core * 4
    theirs = 4 - mine

    def level_of(q):
        return lax.rem(2 * depth - q + (depth - 2) * (q // depth), depth)

    def load(z):
        return pltpu.make_async_copy(dist_ref.at[:, z], raw.at[z], in_sem.at[z])

    def message(kind, lane, q):
        own = lane.coeffs.at[q, mine + chip]
        if kind == CORE_SUM:
            src, dst, target = lane.core_out.at[q], lane.core_in.at[q], to_core
        elif kind == PASS_SUM:
            src, dst, target = lane.a_out.at[q, 0], lane.a_in.at[q, 0], to_a
        elif kind == NEAR_SUM:
            src, dst, target = lane.a_out.at[q, 1], lane.a_in.at[q, 1], to_a
        elif kind == LAST_SUM:
            src, dst, target = lane.b_out.at[q], lane.b_in.at[q], to_b
        elif kind == PAIR_SUM:
            src, dst, target = lane.y_out.at[q], lane.y_in.at[q], to_pair
        elif kind == OUT_B:
            src, dst, target = own, own, to_b
        elif kind == OUT_A:
            src, dst, target = own, own, to_a
        elif kind == OUT_PASS:
            src = lane.coeffs.at[q, mine + chip_b]
            dst, target = src, to_a
        else:
            src = lane.coeffs.at[q, pl.ds(mine, 4)]
            dst, target = src, to_core
        return pltpu.make_async_remote_copy(
            src_ref=src,
            dst_ref=dst,
            send_sem=lane.send.at[kind, q],
            recv_sem=lane.recv.at[kind, q],
            device_id=target,
            device_id_type=MESH,
        )

    def halo(n, x):
        return pltpu.make_async_remote_copy(
            src_ref=state.at[n, 1 + source_plane, x],
            dst_ref=state.at[n, halo_slot, x],
            send_sem=halo_send.at[n, x],
            recv_sem=halo_recv.at[n, x],
            device_id=to_slab,
            device_id_type=MESH,
        )

    def flux(n, k, sender):
        return pltpu.make_async_remote_copy(
            src_ref=flux_out.at[n],
            dst_ref=flux_in.at[n, sender],
            send_sem=flux_send.at[n, k],
            recv_sem=flux_recv.at[n, sender],
            device_id=(slab, (1 - upper) * 8 + k),
            device_id_type=MESH,
        )

    for q in range(depth):
        load((depth - q) % depth).start()

    barrier = pltpu.get_barrier_semaphore()

    def greet(target):
        pl.semaphore_signal(barrier, inc=1, device_id=target, device_id_type=MESH)

    for target in (to_core, to_a, to_b):
        greet(target)
    for k in range(8):
        greet((slab, (1 - upper) * 8 + k))
    greet((lax.rem(slab + slabs - 1, slabs), vel))
    greet((lax.rem(slab + 1, slabs), vel))

    down_t[...] = down_ref[...].T
    for j in range(4):
        for base, left in ((theirs, True), (mine, False)):
            rows = pl.ds(pl.multiple_of((base + j) * 32, 32), 32)
            both = jnp.dot(down_t[rows, :], up_ref[...], preferred_element_type=F32)
            for side in range(2):
                value = both[:, 128 * side : 128 * side + 128]
                if left:
                    extra.core_out[0, j, 32 * side : 32 * side + 32] = value.astype(BF16)
                else:
                    extra.part[0, j, 32 * side : 32 * side + 32] = value
    ids = lax.broadcasted_iota(jnp.int32, (256, 128), 0)
    speed_x = jnp.abs(((ids >> 4).astype(F32) - MIDPOINT) * SPACING)
    speed_y = jnp.abs(((ids & 15).astype(F32) - MIDPOINT) * SPACING)
    speed_z = jnp.abs((vel.astype(F32) - MIDPOINT) * SPACING)
    decay = jnp.concatenate(
        [jnp.broadcast_to(decay_ref[i : i + 1, :], (128, 128)).T for i in range(2)], axis=0
    )
    keep[...] = 1.0 - time_ratio * (speed_x + speed_y + speed_z + decay)
    slope_x[...] = time_ratio * speed_x
    slope_y[...] = time_ratio * speed_y
    slope_z = time_ratio * speed_z

    def arrange(q, carry):
        z = level_of(q)
        load(z).wait()

        def block(i, inner):
            rows = pl.ds(pl.multiple_of(i * 16, 16), 16)
            state[0, 1 + z, :, rows, :] = jnp.swapaxes(raw[z, rows], 0, 1)
            return inner

        return lax.fori_loop(0, 16, block, carry)

    lax.fori_loop(0, depth, arrange, 0)
    pl.semaphore_wait(barrier, 13)

    def send_row(n, x):
        @pl.when(sends_halo)
        def _():
            halo(n, x).start()

    def send_flux(n):
        @pl.when(jnp.logical_not(sends_halo))
        def _():
            for x in range(8):
                plane = state[n, 1 + source_plane, x].astype(F32)
                flux_out[n, x : x + 1, :] = speed_z * jnp.sum(plane, axis=0, keepdims=True)
            for k in range(8):
                flux(n, k, chip * 2 + core).start()

    def take_edge(n):
        @pl.when(takes_halo)
        def _():
            for x in range(8):
                halo(n, x).wait_recv()

        @pl.when(jnp.logical_not(takes_halo))
        def _():
            wall(n)

    def wall(n):
        for k in range(8):
            flux(n, k, k).wait_recv()
        line = (lax.broadcasted_iota(jnp.int32, (8, 128), 1).astype(F32) - MIDPOINT) * SPACING
        valid = lax.broadcasted_iota(jnp.int32, (8, 128), 1) < NV
        gauss = jnp.where(valid, jnp.exp(-0.5 * line * line), 0.0)
        flow = jnp.sum(jnp.maximum(line, 0.0) * gauss, axis=1, keepdims=True)
        mass = jnp.sum(gauss, axis=1, keepdims=True)
        norm = flow * mass * mass
        out = flux_in[n, 0]
        for k in range(1, 8):
            out = out + flux_in[n, k]
        kind = wall_ref[1 - upper]
        opened = jnp.where(kind == 2, 0.0, 1.0)
        sigma = out / norm * opened
        heating = jnp.where(kind == 1, wall_heat, 0.0)
        rows = lax.broadcasted_iota(jnp.int32, (256, 128), 0)
        one_x = ((rows >> 4).astype(F32) - MIDPOINT) * SPACING
        one_y = ((rows & 15).astype(F32) - MIDPOINT) * SPACING
        half_sq = 0.5 * (one_x * one_x + one_y * one_y + speed_z * speed_z)
        maxwell = jnp.exp(-half_sq)
        energy = half_sq - 1.5
        for x in range(8):
            ghost = maxwell * (sigma[x : x + 1] + heating[x : x + 1] * energy)
            state[n, halo_slot, x] = ghost.astype(BF16)

    def drift(n, z, x, half):
        rows = slice(128 * half, 128 * half + 128)
        beside = lax.rem(x + (1 if half == 0 else 7), 8)
        centre = state[n, 1 + z, x, rows].astype(F32)
        wind_z = state[n, 1 + z - sign, x, rows].astype(F32)
        wind_x = state[n, 1 + z, beside, rows].astype(F32)
        split = centre.reshape(8, 16, 128)
        wind_y = jnp.concatenate(
            [pltpu.roll(split[:, :8], 127, 2), pltpu.roll(split[:, 8:], 1, 2)], axis=1
        ).reshape(128, 128)
        return (
            keep[rows] * centre
            + slope_z * wind_z
            + slope_x[rows] * wind_x
            + slope_y[rows] * wind_y
        )

    def begin(q):
        n, z = q // depth, level_of(q)

        @pl.when(q >= depth)
        def _():
            def row(x, carry):
                for half in range(2):
                    rows = slice(128 * half, 128 * half + 128)
                    state[STEPS, 1 + z, x, rows] = drift(0, z, x, half).astype(BF16)
                return carry

            lax.fori_loop(0, 8, row, 0)

        def project(x):
            pair = jnp.concatenate(
                [state[STEPS * n, 1 + z, x], state[STEPS * n, 1 + z, x + 1]], axis=1
            )
            return jnp.dot(down_t[...], pair, preferred_element_type=F32)

        for j in range(2):
            both = project(theirs + 2 * j)
            cells.core_out[q, 2 * j] = both[:, :128].astype(BF16)
            cells.core_out[q, 2 * j + 1] = both[:, 128:].astype(BF16)
        message(CORE_SUM, cells, q).start()
        for j in range(2):
            both = project(mine + 2 * j)
            cells.part[q, 2 * j] = both[:, :128]
            cells.part[q, 2 * j + 1] = both[:, 128:]

    def chip_sum(lane, q, j):
        return lane.part[q, j] + lane.core_in[q, j].astype(F32)

    def first_sums(lane, q):
        message(CORE_SUM, lane, q).wait_recv()
        lane.a_out[q, 0] = chip_sum(lane, q, chip_o).astype(BF16)
        message(PASS_SUM, lane, q).start()
        lane.a_out[q, 1] = chip_sum(lane, q, chip_a).astype(BF16)
        message(NEAR_SUM, lane, q).start()

    def second_sums(lane, q):
        message(PASS_SUM, lane, q).wait_recv()
        total = chip_sum(lane, q, chip_b) + lane.a_in[q, 0].astype(F32)
        lane.b_out[q] = total.astype(BF16)
        message(LAST_SUM, lane, q).start()

    def third_sums(lane, q):
        message(NEAR_SUM, lane, q).wait_recv()
        message(LAST_SUM, lane, q).wait_recv()
        total = chip_sum(lane, q, chip) + lane.a_in[q, 1].astype(F32)
        total = total + lane.b_in[q].astype(F32)
        lane.part[q, chip] = total
        lane.y_out[q] = total.astype(BF16)
        message(PAIR_SUM, lane, q).start()

    def finish_sums(lane, q):
        message(PAIR_SUM, lane, q).wait_recv()
        if lane is cells:

            @pl.when(q >= depth)
            def _():
                before = lax.rem(depth - level_of(q), depth)
                known = lane.coeffs[before, mine + chip]
                gain = jnp.dot(mix[...], known, preferred_element_type=F32)
                lane.part[q, chip] += time_ratio * gain

        total = lane.part[q, chip] + lane.y_in[q].astype(F32)
        lane.coeffs[q, mine + chip] = total.astype(BF16)
        message(OUT_B, lane, q).start()
        message(OUT_A, lane, q).start()

    def pass_on(lane, q):
        message(OUT_B, lane, q).wait_recv()
        message(OUT_PASS, lane, q).start()

    def cross(lane, q):
        message(OUT_A, lane, q).wait_recv()
        message(OUT_PASS, lane, q).wait_recv()
        message(CORE_OUT, lane, q).start()

    def finish_mix():
        message(CORE_OUT, extra, 0).wait_recv()
        for j in range(8):
            for side in range(2):
                piece = extra.coeffs[0, j, 32 * side : 32 * side + 32]
                mix[32 * j : 32 * j + 32, 128 * side : 128 * side + 128] = piece

    def update(q):
        n, z = q // depth, level_of(q)
        message(CORE_OUT, cells, q).wait_recv()

        @pl.when((q >= depth) & (z == target_plane))
        def _():
            take_edge(1)

        def row_pair(i, carry):
            pair = jnp.concatenate([cells.coeffs[q, 2 * i], cells.coeffs[q, 2 * i + 1]], axis=1)
            gained = jnp.dot(up_ref[...], pair, preferred_element_type=F32)
            for side in range(2):
                x = 2 * i + side
                for half in range(2):
                    rows = slice(128 * half, 128 * half + 128)
                    new = (
                        drift(n, z, x, half)
                        + time_ratio * gained[rows, 128 * side : 128 * side + 128]
                    )
                    state[n + 1, 1 + z, x, rows] = new.astype(BF16)
            return carry

        lax.fori_loop(0, 4, row_pair, 0)

        @pl.when((q < depth) & (z == source_plane))
        def _():
            send_flux(1)

        @pl.when(q >= depth)
        def _():
            def block(i, carry):
                rows = pl.ds(pl.multiple_of(i * 16, 16), 16)
                out_ref[rows, z] = jnp.swapaxes(state[STEPS, 1 + z, :, rows, :], 0, 1)
                return carry

            lax.fori_loop(0, 16, block, 0)

    order = [
        (cross, LAG_CROSS),
        (pass_on, LAG_PASS),
        (finish_sums, LAG_FINISH),
        (third_sums, LAG_THIRD),
        (second_sums, LAG_SECOND),
        (first_sums, LAG_FIRST),
    ]

    def tick(t, carry):
        @pl.when(t == LAG_UPDATE)
        def _():
            finish_mix()

        for act, lag in order:

            @pl.when(t == lag)
            def _(act=act):
                act(extra, 0)

            @pl.when((t >= lag) & (t < lag + chunks))
            def _(act=act, lag=lag):
                act(cells, t - lag)

        @pl.when(t < 8)
        def _():
            send_row(0, t)

        @pl.when((t >= LAG_UPDATE + 2) & (t < LAG_UPDATE + 6))
        def _():
            for side in range(2):
                send_row(1, 2 * (t - LAG_UPDATE - 2) + side)

        @pl.when(t == EDGE_TICK)
        def _():
            take_edge(0)

        @pl.when(t >= LAG_UPDATE)
        def _():
            update(t - LAG_UPDATE)

        @pl.when(t < chunks)
        def _():
            begin(t)

        return carry

    message(CORE_SUM, extra, 0).start()
    send_flux(0)
    lax.fori_loop(0, chunks + LAG_UPDATE, tick, 0)

    def drain(q, carry):
        for kind in range(9):
            message(kind, cells, q).wait_send()
        return carry

    lax.fori_loop(0, chunks, drain, 0)
    for kind in range(9):
        message(kind, extra, 0).wait_send()

    @pl.when(sends_halo)
    def _():
        for n in range(STEPS):
            for x in range(8):
                halo(n, x).wait_send()

    @pl.when(jnp.logical_not(sends_halo))
    def _():
        for n in range(STEPS):
            for k in range(8):
                flux(n, k, chip * 2 + core).wait_send()


def lane_shapes(chunks, piece):
    def vmem(lead, kind):
        return pltpu.VMEM((chunks,) + lead + piece, kind)

    return Lane(
        part=vmem((4,), F32),
        core_out=vmem((4,), BF16),
        core_in=vmem((4,), BF16),
        a_out=vmem((2,), BF16),
        a_in=vmem((2,), BF16),
        b_out=vmem((), BF16),
        b_in=vmem((), BF16),
        y_out=vmem((), BF16),
        y_in=vmem((), BF16),
        coeffs=vmem((8,), BF16),
        send=pltpu.SemaphoreType.DMA((9, chunks)),
        recv=pltpu.SemaphoreType.DMA((9, chunks)),
    )


def body(slabs, distribution, up_factor, down_factor, decay, wall_kind):
    local_vel, depth, width_x, width_y = distribution.shape
    rank = up_factor.shape[1]
    vmem = pl.BlockSpec(memory_space=pltpu.VMEM)
    anywhere = pl.BlockSpec(memory_space=pl.ANY)
    dma = pltpu.SemaphoreType.DMA
    return pl.pallas_call(
        functools.partial(kernel, depth, slabs),
        out_shape=pltpu.VMEM(distribution.shape, distribution.dtype),
        in_specs=[anywhere, vmem, vmem, vmem, vmem],
        out_specs=vmem,
        scratch_shapes=[
            pltpu.VMEM((STEPS + 1, depth + 2, width_x, local_vel, width_y), BF16),
            pltpu.VMEM((depth, local_vel, width_x, width_y), BF16),
            pltpu.VMEM((rank, local_vel), BF16),
            pltpu.VMEM((rank, rank), BF16),
            pltpu.VMEM((local_vel, width_y), F32),
            pltpu.VMEM((local_vel, width_y), F32),
            pltpu.VMEM((local_vel, width_y), F32),
            pltpu.VMEM((STEPS, width_x, width_y), F32),
            pltpu.VMEM((STEPS, 8, width_x, width_y), F32),
            dma((STEPS, 8)),
            dma((STEPS, 8)),
            dma((STEPS, 8)),
            dma((STEPS, 8)),
            dma((depth,)),
            *lane_shapes(STEPS * depth, (rank, width_y)),
            *lane_shapes(1, (rank // 4, width_y)),
        ],
        compiler_params=pltpu.CompilerParams(
            collective_id=0, has_side_effects=True, vmem_limit_bytes=VMEM_MIB * 2**20
        ),
        cost_estimate=pl.CostEstimate(
            flops=4 * STEPS * local_vel * rank * depth * width_x * width_y,
            bytes_accessed=4 * distribution.size,
            transcendentals=0,
        ),
        name="boltzmann_steps",
    )(distribution, up_factor, down_factor, decay.reshape(2, -1), wall_kind)


def solution(mesh):
    return jax.shard_map(
        functools.partial(body, mesh.shape["space"]),
        mesh=mesh,
        in_specs=(P("vel", "space", None, None), P("vel", None), P("vel", None), P("vel"), P()),
        out_specs=P("vel", "space", None, None),
        check_vma=False,
    )
```

```python
import functools
from typing import Any, NamedTuple

import jax
import jax.numpy as jnp
from jax import lax
from jax.experimental import pallas as pl
from jax.experimental.pallas import tpu as pltpu
from jax.sharding import PartitionSpec as P

NV = 16
STEPS = 2
MESH = pl.DeviceIdType.MESH
VMEM_MIB = 56

speed_range = 8.0
time_ratio = 0.08
wall_heat = 3.0

SPACING = speed_range / NV
MIDPOINT = (NV - 1) / 2.0
F32 = jnp.float32
BF16 = jnp.bfloat16

CORE_SUM, PASS_SUM, NEAR_SUM, LAST_SUM, PAIR_SUM, OUT_B, OUT_A, OUT_PASS, CORE_OUT = range(9)
LAG_FIRST, LAG_SECOND, LAG_THIRD, LAG_FINISH, LAG_PASS, LAG_CROSS, LAG_UPDATE = (
    1, 3, 6, 9, 12, 14, 15,
)
EDGE_TICK = 9


class Lane(NamedTuple):
    part: Any
    core_out: Any
    core_in: Any
    a_out: Any
    a_in: Any
    b_out: Any
    b_in: Any
    y_out: Any
    y_in: Any
    coeffs: Any
    send: Any
    recv: Any


def kernel(
    depth,
    slabs,
    dist_ref,
    up_ref,
    down_ref,
    decay_ref,
    wall_ref,
    out_ref,
    state,
    raw,
    down_t,
    mix,
    keep,
    slope_x,
    slope_y,
    flux_out,
    flux_in,
    halo_send,
    halo_recv,
    flux_send,
    flux_recv,
    in_sem,
    *lane_refs,
):
    count = len(Lane._fields)
    cells = Lane(*lane_refs[:count])
    extra = Lane(*lane_refs[count:])
    chunks = STEPS * depth
    slab = lax.axis_index("space")
    vel = lax.axis_index("vel")
    core = lax.rem(vel, 2)
    chip = lax.rem(vel // 2, 4)
    upper = vel // 8
    sign = 2 * upper - 1
    flip = chip + 1 - 2 * lax.rem(chip, 2)
    mirror = 3 - chip
    chip_a = flip * (1 - core) + mirror * core
    chip_b = mirror * (1 - core) + flip * core
    chip_o = lax.rem(chip + 2, 4)

    def device(pair, x, c):
        return (slab, pair * 8 + x * 2 + c)

    to_core = device(upper, chip, 1 - core)
    to_a = device(upper, chip_a, core)
    to_b = device(upper, chip_b, core)
    to_pair = device(1 - upper, chip, core)
    to_slab = (lax.rem(slab + sign + slabs, slabs), vel)
    last = depth - 1
    source_plane = last * upper
    target_plane = last * (1 - upper)
    halo_slot = (depth + 1) * (1 - upper)
    sends_halo = slab != (slabs - 1) * upper
    takes_halo = slab != (slabs - 1) * (1 - upper)
    mine = core * 4
    theirs = 4 - mine

    def level_of(q):
        return lax.rem(2 * depth - q + (depth - 2) * (q // depth), depth)

    def load(z):
        return pltpu.make_async_copy(dist_ref.at[:, z], raw.at[z], in_sem.at[z])

    def message(kind, lane, q):
        own = lane.coeffs.at[q, mine + chip]
        if kind == CORE_SUM:
            src, dst, target = lane.core_out.at[q], lane.core_in.at[q], to_core
        elif kind == PASS_SUM:
            src, dst, target = lane.a_out.at[q, 0], lane.a_in.at[q, 0], to_a
        elif kind == NEAR_SUM:
            src, dst, target = lane.a_out.at[q, 1], lane.a_in.at[q, 1], to_a
        elif kind == LAST_SUM:
            src, dst, target = lane.b_out.at[q], lane.b_in.at[q], to_b
        elif kind == PAIR_SUM:
            src, dst, target = lane.y_out.at[q], lane.y_in.at[q], to_pair
        elif kind == OUT_B:
            src, dst, target = own, own, to_b
        elif kind == OUT_A:
            src, dst, target = own, own, to_a
        elif kind == OUT_PASS:
            src = lane.coeffs.at[q, mine + chip_b]
            dst, target = src, to_a
        else:
            src = lane.coeffs.at[q, pl.ds(mine, 4)]
            dst, target = src, to_core
        return pltpu.make_async_remote_copy(
            src_ref=src,
            dst_ref=dst,
            send_sem=lane.send.at[kind, q],
            recv_sem=lane.recv.at[kind, q],
            device_id=target,
            device_id_type=MESH,
        )

    def halo(n, x):
        return pltpu.make_async_remote_copy(
            src_ref=state.at[n, 1 + source_plane, x],
            dst_ref=state.at[n, halo_slot, x],
            send_sem=halo_send.at[n, x],
            recv_sem=halo_recv.at[n, x],
            device_id=to_slab,
            device_id_type=MESH,
        )

    def flux(n, k, sender):
        return pltpu.make_async_remote_copy(
            src_ref=flux_out.at[n],
            dst_ref=flux_in.at[n, sender],
            send_sem=flux_send.at[n, k],
            recv_sem=flux_recv.at[n, sender],
            device_id=(slab, (1 - upper) * 8 + k),
            device_id_type=MESH,
        )

    for q in range(depth):
        load((depth - q) % depth).start()

    barrier = pltpu.get_barrier_semaphore()

    def greet(target):
        pl.semaphore_signal(barrier, inc=1, device_id=target, device_id_type=MESH)

    for target in (to_core, to_a, to_b, to_pair):
        greet(target)

    @pl.when(takes_halo)
    def _():
        greet((slab - sign, vel))

    @pl.when(jnp.logical_not(takes_halo))
    def _():
        for k in range(1, 8):
            greet((slab, (1 - upper) * 8 + lax.rem(chip * 2 + core + k, 8)))

    down_t[...] = down_ref[...].T
    for j in range(4):
        for base, left in ((theirs, True), (mine, False)):
            rows = pl.ds(pl.multiple_of((base + j) * 32, 32), 32)
            both = jnp.dot(down_t[rows, :], up_ref[...], preferred_element_type=F32)
            for side in range(2):
                value = both[:, 128 * side : 128 * side + 128]
                if left:
                    extra.core_out[0, j, 32 * side : 32 * side + 32] = value.astype(BF16)
                else:
                    extra.part[0, j, 32 * side : 32 * side + 32] = value
    ids = lax.broadcasted_iota(jnp.int32, (256, 128), 0)
    speed_x = jnp.abs(((ids >> 4).astype(F32) - MIDPOINT) * SPACING)
    speed_y = jnp.abs(((ids & 15).astype(F32) - MIDPOINT) * SPACING)
    speed_z = jnp.abs((vel.astype(F32) - MIDPOINT) * SPACING)
    decay = jnp.concatenate(
        [jnp.broadcast_to(decay_ref[i : i + 1, :], (128, 128)).T for i in range(2)], axis=0
    )
    keep[...] = 1.0 - time_ratio * (speed_x + speed_y + speed_z + decay)
    slope_x[...] = time_ratio * speed_x
    slope_y[...] = time_ratio * speed_y
    slope_z = time_ratio * speed_z

    def arrange(q, carry):
        z = level_of(q)
        load(z).wait()

        def block(i, inner):
            rows = pl.ds(pl.multiple_of(i * 16, 16), 16)
            state[0, 1 + z, :, rows, :] = jnp.swapaxes(raw[z, rows], 0, 1)
            return inner

        return lax.fori_loop(0, 16, block, carry)

    lax.fori_loop(0, depth, arrange, 0)

    def send_row(n, x):
        @pl.when(sends_halo)
        def _():
            halo(n, x).start()

    def send_flux(n):
        @pl.when(jnp.logical_not(sends_halo))
        def _():
            for x in range(8):
                plane = state[n, 1 + source_plane, x].astype(F32)
                flux_out[n, x : x + 1, :] = speed_z * jnp.sum(plane, axis=0, keepdims=True)
            for k in range(8):
                flux(n, k, chip * 2 + core).start()

    def take_edge(n):
        @pl.when(takes_halo)
        def _():
            for x in range(8):
                halo(n, x).wait_recv()

        @pl.when(jnp.logical_not(takes_halo))
        def _():
            wall(n)

    def wall(n):
        for k in range(8):
            flux(n, k, k).wait_recv()
        line = (lax.broadcasted_iota(jnp.int32, (8, 128), 1).astype(F32) - MIDPOINT) * SPACING
        valid = lax.broadcasted_iota(jnp.int32, (8, 128), 1) < NV
        gauss = jnp.where(valid, jnp.exp(-0.5 * line * line), 0.0)
        flow = jnp.sum(jnp.maximum(line, 0.0) * gauss, axis=1, keepdims=True)
        mass = jnp.sum(gauss, axis=1, keepdims=True)
        norm = flow * mass * mass
        out = flux_in[n, 0]
        for k in range(1, 8):
            out = out + flux_in[n, k]
        kind = wall_ref[1 - upper]
        opened = jnp.where(kind == 2, 0.0, 1.0)
        sigma = out / norm * opened
        heating = jnp.where(kind == 1, wall_heat, 0.0)
        rows = lax.broadcasted_iota(jnp.int32, (256, 128), 0)
        one_x = ((rows >> 4).astype(F32) - MIDPOINT) * SPACING
        one_y = ((rows & 15).astype(F32) - MIDPOINT) * SPACING
        half_sq = 0.5 * (one_x * one_x + one_y * one_y + speed_z * speed_z)
        maxwell = jnp.exp(-half_sq)
        energy = half_sq - 1.5
        for x in range(8):
            ghost = maxwell * (sigma[x : x + 1] + heating[x : x + 1] * energy)
            state[n, halo_slot, x] = ghost.astype(BF16)

    def drift(n, z, x, half):
        rows = slice(128 * half, 128 * half + 128)
        beside = lax.rem(x + (1 if half == 0 else 7), 8)
        centre = state[n, 1 + z, x, rows].astype(F32)
        wind_z = state[n, 1 + z - sign, x, rows].astype(F32)
        wind_x = state[n, 1 + z, beside, rows].astype(F32)
        split = centre.reshape(8, 16, 128)
        wind_y = jnp.concatenate(
            [pltpu.roll(split[:, :8], 127, 2), pltpu.roll(split[:, 8:], 1, 2)], axis=1
        ).reshape(128, 128)
        return (
            keep[rows] * centre
            + slope_z * wind_z
            + slope_x[rows] * wind_x
            + slope_y[rows] * wind_y
        )

    def begin(q):
        n, z = q // depth, level_of(q)

        @pl.when(q >= depth)
        def _():
            def row(x, carry):
                for half in range(2):
                    rows = slice(128 * half, 128 * half + 128)
                    state[STEPS, 1 + z, x, rows] = drift(0, z, x, half).astype(BF16)
                return carry

            lax.fori_loop(0, 8, row, 0)

        def project(x):
            pair = jnp.concatenate(
                [state[STEPS * n, 1 + z, x], state[STEPS * n, 1 + z, x + 1]], axis=1
            )
            return jnp.dot(down_t[...], pair, preferred_element_type=F32)

        for j in range(2):
            both = project(theirs + 2 * j)
            cells.core_out[q, 2 * j] = both[:, :128].astype(BF16)
            cells.core_out[q, 2 * j + 1] = both[:, 128:].astype(BF16)
        for j in range(2):
            both = project(mine + 2 * j)
            cells.part[q, 2 * j] = both[:, :128]
            cells.part[q, 2 * j + 1] = both[:, 128:]

    def chip_sum(lane, q, j):
        return lane.part[q, j] + lane.core_in[q, j].astype(F32)

    def first_sums(lane, q):
        message(CORE_SUM, lane, q).wait_recv()
        lane.a_out[q, 0] = chip_sum(lane, q, chip_o).astype(BF16)
        message(PASS_SUM, lane, q).start()
        lane.a_out[q, 1] = chip_sum(lane, q, chip_a).astype(BF16)
        message(NEAR_SUM, lane, q).start()

    def second_sums(lane, q):
        message(PASS_SUM, lane, q).wait_recv()
        total = chip_sum(lane, q, chip_b) + lane.a_in[q, 0].astype(F32)
        lane.b_out[q] = total.astype(BF16)
        message(LAST_SUM, lane, q).start()

    def third_sums(lane, q):
        message(NEAR_SUM, lane, q).wait_recv()
        message(LAST_SUM, lane, q).wait_recv()
        total = chip_sum(lane, q, chip) + lane.a_in[q, 1].astype(F32)
        total = total + lane.b_in[q].astype(F32)
        lane.part[q, chip] = total
        lane.y_out[q] = total.astype(BF16)
        message(PAIR_SUM, lane, q).start()

    def finish_sums(lane, q):
        message(PAIR_SUM, lane, q).wait_recv()
        if lane is cells:

            @pl.when(q >= depth)
            def _():
                before = lax.rem(depth - level_of(q), depth)
                known = lane.coeffs[before, mine + chip]
                gain = jnp.dot(mix[...], known, preferred_element_type=F32)
                lane.part[q, chip] += time_ratio * gain

        total = lane.part[q, chip] + lane.y_in[q].astype(F32)
        lane.coeffs[q, mine + chip] = total.astype(BF16)
        message(OUT_B, lane, q).start()
        message(OUT_A, lane, q).start()

    def pass_on(lane, q):
        message(OUT_B, lane, q).wait_recv()
        message(OUT_PASS, lane, q).start()

    def cross(lane, q):
        message(OUT_A, lane, q).wait_recv()
        message(OUT_PASS, lane, q).wait_recv()
        message(CORE_OUT, lane, q).start()

    def finish_mix():
        message(CORE_OUT, extra, 0).wait_recv()
        for j in range(8):
            for side in range(2):
                piece = extra.coeffs[0, j, 32 * side : 32 * side + 32]
                mix[32 * j : 32 * j + 32, 128 * side : 128 * side + 128] = piece

    def update(q):
        n, z = q // depth, level_of(q)
        message(CORE_OUT, cells, q).wait_recv()

        @pl.when((q >= depth) & (z == target_plane))
        def _():
            take_edge(1)

        def row_pair(i, carry):
            pair = jnp.concatenate([cells.coeffs[q, 2 * i], cells.coeffs[q, 2 * i + 1]], axis=1)
            gained = jnp.dot(up_ref[...], pair, preferred_element_type=F32)
            for side in range(2):
                x = 2 * i + side
                for half in range(2):
                    rows = slice(128 * half, 128 * half + 128)
                    new = (
                        drift(n, z, x, half)
                        + time_ratio * gained[rows, 128 * side : 128 * side + 128]
                    )
                    state[n + 1, 1 + z, x, rows] = new.astype(BF16)
            return carry

        lax.fori_loop(0, 4, row_pair, 0)

        @pl.when((q < depth) & (z == source_plane))
        def _():
            send_flux(1)

        @pl.when(q >= depth)
        def _():
            def block(i, carry):
                rows = pl.ds(pl.multiple_of(i * 16, 16), 16)
                out_ref[rows, z] = jnp.swapaxes(state[STEPS, 1 + z, :, rows, :], 0, 1)
                return carry

            lax.fori_loop(0, 16, block, 0)

    order = [
        (cross, LAG_CROSS),
        (pass_on, LAG_PASS),
        (finish_sums, LAG_FINISH),
        (third_sums, LAG_THIRD),
        (second_sums, LAG_SECOND),
        (first_sums, LAG_FIRST),
    ]

    def tick(t, carry):
        @pl.when(t < chunks)
        def _():
            message(CORE_SUM, cells, t).start()

        @pl.when(t == LAG_UPDATE)
        def _():
            finish_mix()

        for act, lag in order:

            @pl.when(t == lag)
            def _(act=act):
                act(extra, 0)

            @pl.when((t >= lag) & (t < lag + chunks))
            def _(act=act, lag=lag):
                act(cells, t - lag)

        @pl.when(t < 8)
        def _():
            send_row(0, t)

        @pl.when((t >= LAG_UPDATE + 2) & (t < LAG_UPDATE + 6))
        def _():
            for side in range(2):
                send_row(1, 2 * (t - LAG_UPDATE - 2) + side)

        @pl.when(t == EDGE_TICK)
        def _():
            take_edge(0)

        @pl.when(t >= LAG_UPDATE)
        def _():
            update(t - LAG_UPDATE)

        @pl.when(t < chunks - 1)
        def _():
            begin(t + 1)

        return carry

    begin(0)
    pl.semaphore_wait(barrier, jnp.where(sends_halo, 5, 11))
    message(CORE_SUM, extra, 0).start()
    send_flux(0)
    lax.fori_loop(0, chunks + LAG_UPDATE, tick, 0)

    def drain(q, carry):
        for kind in range(9):
            message(kind, cells, q).wait_send()
        return carry

    lax.fori_loop(0, chunks, drain, 0)
    for kind in range(9):
        message(kind, extra, 0).wait_send()

    @pl.when(sends_halo)
    def _():
        for n in range(STEPS):
            for x in range(8):
                halo(n, x).wait_send()

    @pl.when(jnp.logical_not(sends_halo))
    def _():
        for n in range(STEPS):
            for k in range(8):
                flux(n, k, chip * 2 + core).wait_send()


def lane_shapes(chunks, piece):
    def vmem(lead, kind):
        return pltpu.VMEM((chunks,) + lead + piece, kind)

    return Lane(
        part=vmem((4,), F32),
        core_out=vmem((4,), BF16),
        core_in=vmem((4,), BF16),
        a_out=vmem((2,), BF16),
        a_in=vmem((2,), BF16),
        b_out=vmem((), BF16),
        b_in=vmem((), BF16),
        y_out=vmem((), BF16),
        y_in=vmem((), BF16),
        coeffs=vmem((8,), BF16),
        send=pltpu.SemaphoreType.DMA((9, chunks)),
        recv=pltpu.SemaphoreType.DMA((9, chunks)),
    )


def body(slabs, distribution, up_factor, down_factor, decay, wall_kind):
    local_vel, depth, width_x, width_y = distribution.shape
    rank = up_factor.shape[1]
    vmem = pl.BlockSpec(memory_space=pltpu.VMEM)
    anywhere = pl.BlockSpec(memory_space=pl.ANY)
    dma = pltpu.SemaphoreType.DMA
    return pl.pallas_call(
        functools.partial(kernel, depth, slabs),
        out_shape=pltpu.VMEM(distribution.shape, distribution.dtype),
        in_specs=[anywhere, vmem, vmem, vmem, vmem],
        out_specs=vmem,
        scratch_shapes=[
            pltpu.VMEM((STEPS + 1, depth + 2, width_x, local_vel, width_y), BF16),
            pltpu.VMEM((depth, local_vel, width_x, width_y), BF16),
            pltpu.VMEM((rank, local_vel), BF16),
            pltpu.VMEM((rank, rank), BF16),
            pltpu.VMEM((local_vel, width_y), F32),
            pltpu.VMEM((local_vel, width_y), F32),
            pltpu.VMEM((local_vel, width_y), F32),
            pltpu.VMEM((STEPS, width_x, width_y), F32),
            pltpu.VMEM((STEPS, 8, width_x, width_y), F32),
            dma((STEPS, 8)),
            dma((STEPS, 8)),
            dma((STEPS, 8)),
            dma((STEPS, 8)),
            dma((depth,)),
            *lane_shapes(STEPS * depth, (rank, width_y)),
            *lane_shapes(1, (rank // 4, width_y)),
        ],
        compiler_params=pltpu.CompilerParams(
            collective_id=0, has_side_effects=True, vmem_limit_bytes=VMEM_MIB * 2**20
        ),
        cost_estimate=pl.CostEstimate(
            flops=4 * STEPS * local_vel * rank * depth * width_x * width_y,
            bytes_accessed=4 * distribution.size,
            transcendentals=0,
        ),
        name="boltzmann_steps",
    )(distribution, up_factor, down_factor, decay.reshape(2, -1), wall_kind)


def solution(mesh):
    return jax.shard_map(
        functools.partial(body, mesh.shape["space"]),
        mesh=mesh,
        in_specs=(P("vel", "space", None, None), P("vel", None), P("vel", None), P("vel"), P()),
        out_specs=P("vel", "space", None, None),
        check_vma=False,
    )
```

```python
import functools
from typing import Any, NamedTuple

import jax
import jax.numpy as jnp
from jax import lax
from jax.experimental import pallas as pl
from jax.experimental.pallas import tpu as pltpu
from jax.sharding import PartitionSpec as P

NV = 16
STEPS = 2
MESH = pl.DeviceIdType.MESH
VMEM_MIB = 56

speed_range = 8.0
time_ratio = 0.08
wall_heat = 3.0

SPACING = speed_range / NV
MIDPOINT = (NV - 1) / 2.0
F32 = jnp.float32
BF16 = jnp.bfloat16

CORE_SUM, PASS_SUM, NEAR_SUM, LAST_SUM, PAIR_SUM, OUT_B, OUT_A, OUT_PASS, CORE_OUT = range(9)
LAG_FIRST, LAG_SECOND, LAG_THIRD, LAG_FINISH, LAG_PASS, LAG_CROSS, LAG_UPDATE = (
    0, 2, 5, 8, 11, 13, 14,
)
EDGE_TICK = 8
AHEAD = 2


class Lane(NamedTuple):
    part: Any
    core_out: Any
    core_in: Any
    a_out: Any
    a_in: Any
    b_out: Any
    b_in: Any
    y_out: Any
    y_in: Any
    coeffs: Any
    send: Any
    recv: Any


def kernel(
    depth,
    slabs,
    dist_ref,
    up_ref,
    down_ref,
    decay_ref,
    wall_ref,
    out_ref,
    state,
    raw,
    down_t,
    mix,
    keep,
    slope_x,
    slope_y,
    flux_out,
    flux_in,
    halo_send,
    halo_recv,
    flux_send,
    flux_recv,
    in_sem,
    *lane_refs,
):
    count = len(Lane._fields)
    cells = Lane(*lane_refs[:count])
    extra = Lane(*lane_refs[count:])
    chunks = STEPS * depth
    slab = lax.axis_index("space")
    vel = lax.axis_index("vel")
    core = lax.rem(vel, 2)
    chip = lax.rem(vel // 2, 4)
    upper = vel // 8
    sign = 2 * upper - 1
    flip = chip + 1 - 2 * lax.rem(chip, 2)
    mirror = 3 - chip
    chip_a = flip * (1 - core) + mirror * core
    chip_b = mirror * (1 - core) + flip * core
    chip_o = lax.rem(chip + 2, 4)

    def device(pair, x, c):
        return (slab, pair * 8 + x * 2 + c)

    to_core = device(upper, chip, 1 - core)
    to_a = device(upper, chip_a, core)
    to_b = device(upper, chip_b, core)
    to_pair = device(1 - upper, chip, core)
    to_slab = (lax.rem(slab + sign + slabs, slabs), vel)
    last = depth - 1
    source_plane = last * upper
    target_plane = last * (1 - upper)
    halo_slot = (depth + 1) * (1 - upper)
    sends_halo = slab != (slabs - 1) * upper
    takes_halo = slab != (slabs - 1) * (1 - upper)
    mine = core * 4
    theirs = 4 - mine

    def level_of(q):
        return lax.rem(2 * depth - q + (depth - 2) * (q // depth), depth)

    def load(z):
        return pltpu.make_async_copy(dist_ref.at[:, z], raw.at[z], in_sem.at[z])

    def message(kind, lane, q):
        own = lane.coeffs.at[q, mine + chip]
        if kind == CORE_SUM:
            src, dst, target = lane.core_out.at[q], lane.core_in.at[q], to_core
        elif kind == PASS_SUM:
            src, dst, target = lane.a_out.at[q, 0], lane.a_in.at[q, 0], to_a
        elif kind == NEAR_SUM:
            src, dst, target = lane.a_out.at[q, 1], lane.a_in.at[q, 1], to_a
        elif kind == LAST_SUM:
            src, dst, target = lane.b_out.at[q], lane.b_in.at[q], to_b
        elif kind == PAIR_SUM:
            src, dst, target = lane.y_out.at[q], lane.y_in.at[q], to_pair
        elif kind == OUT_B:
            src, dst, target = own, own, to_b
        elif kind == OUT_A:
            src, dst, target = own, own, to_a
        elif kind == OUT_PASS:
            src = lane.coeffs.at[q, mine + chip_b]
            dst, target = src, to_a
        else:
            src = lane.coeffs.at[q, pl.ds(mine, 4)]
            dst, target = src, to_core
        return pltpu.make_async_remote_copy(
            src_ref=src,
            dst_ref=dst,
            send_sem=lane.send.at[kind, q],
            recv_sem=lane.recv.at[kind, q],
            device_id=target,
            device_id_type=MESH,
        )

    def halo(n, x):
        return pltpu.make_async_remote_copy(
            src_ref=state.at[n, 1 + source_plane, x],
            dst_ref=state.at[n, halo_slot, x],
            send_sem=halo_send.at[n, x],
            recv_sem=halo_recv.at[n, x],
            device_id=to_slab,
            device_id_type=MESH,
        )

    def flux(n, k, sender):
        return pltpu.make_async_remote_copy(
            src_ref=flux_out.at[n],
            dst_ref=flux_in.at[n, sender],
            send_sem=flux_send.at[n, k],
            recv_sem=flux_recv.at[n, sender],
            device_id=(slab, (1 - upper) * 8 + k),
            device_id_type=MESH,
        )

    barrier = pltpu.get_barrier_semaphore()

    def greet(target):
        pl.semaphore_signal(barrier, inc=1, device_id=target, device_id_type=MESH)

    for target in (to_core, to_a, to_b, to_pair):
        greet(target)

    @pl.when(takes_halo)
    def _():
        greet((slab - sign, vel))

    @pl.when(jnp.logical_not(takes_halo))
    def _():
        for k in range(1, 8):
            greet((slab, (1 - upper) * 8 + lax.rem(chip * 2 + core + k, 8)))

    for q in range(depth):
        load((depth - q) % depth).start()

    down_t[...] = down_ref[...].T
    for j in range(4):
        for base, left in ((theirs, True), (mine, False)):
            rows = pl.ds(pl.multiple_of((base + j) * 32, 32), 32)
            both = jnp.dot(down_t[rows, :], up_ref[...], preferred_element_type=F32)
            for side in range(2):
                value = both[:, 128 * side : 128 * side + 128]
                if left:
                    extra.core_out[0, j, 32 * side : 32 * side + 32] = value.astype(BF16)
                else:
                    extra.part[0, j, 32 * side : 32 * side + 32] = value
    ids = lax.broadcasted_iota(jnp.int32, (256, 128), 0)
    speed_x = jnp.abs(((ids >> 4).astype(F32) - MIDPOINT) * SPACING)
    speed_y = jnp.abs(((ids & 15).astype(F32) - MIDPOINT) * SPACING)
    speed_z = jnp.abs((vel.astype(F32) - MIDPOINT) * SPACING)
    decay = jnp.concatenate(
        [jnp.broadcast_to(decay_ref[i : i + 1, :], (128, 128)).T for i in range(2)], axis=0
    )
    keep[...] = 1.0 - time_ratio * (speed_x + speed_y + speed_z + decay)
    slope_x[...] = time_ratio * speed_x
    slope_y[...] = time_ratio * speed_y
    slope_z = time_ratio * speed_z

    def arrange(q, carry):
        z = level_of(q)
        load(z).wait()

        def block(i, inner):
            rows = pl.ds(pl.multiple_of(i * 16, 16), 16)
            state[0, 1 + z, :, rows, :] = jnp.swapaxes(raw[z, rows], 0, 1)
            return inner

        return lax.fori_loop(0, 16, block, carry)

    lax.fori_loop(0, depth, arrange, 0)

    def send_row(n, x):
        @pl.when(sends_halo)
        def _():
            halo(n, x).start()

    def send_flux(n):
        @pl.when(jnp.logical_not(sends_halo))
        def _():
            for x in range(8):
                plane = state[n, 1 + source_plane, x].astype(F32)
                flux_out[n, x : x + 1, :] = speed_z * jnp.sum(plane, axis=0, keepdims=True)
            for k in range(8):
                flux(n, k, chip * 2 + core).start()

    def take_edge(n):
        @pl.when(takes_halo)
        def _():
            for x in range(8):
                halo(n, x).wait_recv()

        @pl.when(jnp.logical_not(takes_halo))
        def _():
            wall(n)

    def wall(n):
        for k in range(8):
            flux(n, k, k).wait_recv()
        line = (lax.broadcasted_iota(jnp.int32, (8, 128), 1).astype(F32) - MIDPOINT) * SPACING
        valid = lax.broadcasted_iota(jnp.int32, (8, 128), 1) < NV
        gauss = jnp.where(valid, jnp.exp(-0.5 * line * line), 0.0)
        flow = jnp.sum(jnp.maximum(line, 0.0) * gauss, axis=1, keepdims=True)
        mass = jnp.sum(gauss, axis=1, keepdims=True)
        norm = flow * mass * mass
        out = flux_in[n, 0]
        for k in range(1, 8):
            out = out + flux_in[n, k]
        kind = wall_ref[1 - upper]
        opened = jnp.where(kind == 2, 0.0, 1.0)
        sigma = out / norm * opened
        heating = jnp.where(kind == 1, wall_heat, 0.0)
        rows = lax.broadcasted_iota(jnp.int32, (256, 128), 0)
        one_x = ((rows >> 4).astype(F32) - MIDPOINT) * SPACING
        one_y = ((rows & 15).astype(F32) - MIDPOINT) * SPACING
        half_sq = 0.5 * (one_x * one_x + one_y * one_y + speed_z * speed_z)
        maxwell = jnp.exp(-half_sq)
        energy = half_sq - 1.5
        for x in range(8):
            ghost = maxwell * (sigma[x : x + 1] + heating[x : x + 1] * energy)
            state[n, halo_slot, x] = ghost.astype(BF16)

    def drift(n, z, x, half):
        rows = slice(128 * half, 128 * half + 128)
        beside = lax.rem(x + (1 if half == 0 else 7), 8)
        centre = state[n, 1 + z, x, rows].astype(F32)
        wind_z = state[n, 1 + z - sign, x, rows].astype(F32)
        wind_x = state[n, 1 + z, beside, rows].astype(F32)
        split = centre.reshape(8, 16, 128)
        wind_y = jnp.concatenate(
            [pltpu.roll(split[:, :8], 127, 2), pltpu.roll(split[:, 8:], 1, 2)], axis=1
        ).reshape(128, 128)
        return (
            keep[rows] * centre
            + slope_z * wind_z
            + slope_x[rows] * wind_x
            + slope_y[rows] * wind_y
        )

    def begin(q):
        n, z = q // depth, level_of(q)

        @pl.when(q >= depth)
        def _():
            def row(x, carry):
                for half in range(2):
                    rows = slice(128 * half, 128 * half + 128)
                    state[STEPS, 1 + z, x, rows] = drift(0, z, x, half).astype(BF16)
                return carry

            lax.fori_loop(0, 8, row, 0)

        def project(x):
            pair = jnp.concatenate(
                [state[STEPS * n, 1 + z, x], state[STEPS * n, 1 + z, x + 1]], axis=1
            )
            return jnp.dot(down_t[...], pair, preferred_element_type=F32)

        for j in range(2):
            both = project(theirs + 2 * j)
            cells.core_out[q, 2 * j] = both[:, :128].astype(BF16)
            cells.core_out[q, 2 * j + 1] = both[:, 128:].astype(BF16)
        for j in range(2):
            both = project(mine + 2 * j)
            cells.part[q, 2 * j] = both[:, :128]
            cells.part[q, 2 * j + 1] = both[:, 128:]

    def chip_sum(lane, q, j):
        return lane.part[q, j] + lane.core_in[q, j].astype(F32)

    def first_sums(lane, q):
        message(CORE_SUM, lane, q).wait_recv()
        lane.a_out[q, 0] = chip_sum(lane, q, chip_o).astype(BF16)
        message(PASS_SUM, lane, q).start()
        lane.a_out[q, 1] = chip_sum(lane, q, chip_a).astype(BF16)
        message(NEAR_SUM, lane, q).start()

    def second_sums(lane, q):
        message(PASS_SUM, lane, q).wait_recv()
        total = chip_sum(lane, q, chip_b) + lane.a_in[q, 0].astype(F32)
        lane.b_out[q] = total.astype(BF16)
        message(LAST_SUM, lane, q).start()

    def third_sums(lane, q):
        message(NEAR_SUM, lane, q).wait_recv()
        message(LAST_SUM, lane, q).wait_recv()
        total = chip_sum(lane, q, chip) + lane.a_in[q, 1].astype(F32)
        total = total + lane.b_in[q].astype(F32)
        lane.part[q, chip] = total
        lane.y_out[q] = total.astype(BF16)
        message(PAIR_SUM, lane, q).start()

    def finish_sums(lane, q):
        message(PAIR_SUM, lane, q).wait_recv()
        if lane is cells:

            @pl.when(q >= depth)
            def _():
                before = lax.rem(depth - level_of(q), depth)
                known = lane.coeffs[before, mine + chip]
                gain = jnp.dot(mix[...], known, preferred_element_type=F32)
                lane.part[q, chip] += time_ratio * gain

        total = lane.part[q, chip] + lane.y_in[q].astype(F32)
        lane.coeffs[q, mine + chip] = total.astype(BF16)
        message(OUT_B, lane, q).start()
        message(OUT_A, lane, q).start()

    def pass_on(lane, q):
        message(OUT_B, lane, q).wait_recv()
        message(OUT_PASS, lane, q).start()

    def cross(lane, q):
        message(OUT_A, lane, q).wait_recv()
        message(OUT_PASS, lane, q).wait_recv()
        message(CORE_OUT, lane, q).start()

    def finish_mix():
        message(CORE_OUT, extra, 0).wait_recv()
        for j in range(8):
            for side in range(2):
                piece = extra.coeffs[0, j, 32 * side : 32 * side + 32]
                mix[32 * j : 32 * j + 32, 128 * side : 128 * side + 128] = piece

    def update_rows(q, base):
        n, z = q // depth, level_of(q)

        def row_pair(i, carry):
            first = base + 2 * i
            pair = jnp.concatenate([cells.coeffs[q, first], cells.coeffs[q, first + 1]], axis=1)
            gained = jnp.dot(up_ref[...], pair, preferred_element_type=F32)
            for side in range(2):
                x = first + side
                for half in range(2):
                    rows = slice(128 * half, 128 * half + 128)
                    new = (
                        drift(n, z, x, half)
                        + time_ratio * gained[rows, 128 * side : 128 * side + 128]
                    )
                    state[n + 1, 1 + z, x, rows] = new.astype(BF16)
            return carry

        lax.fori_loop(0, 2, row_pair, 0)

    def update_own(q):
        @pl.when((q >= depth) & (level_of(q) == target_plane))
        def _():
            take_edge(1)

        update_rows(q, mine)

    def update_rest(q):
        z = level_of(q)
        message(CORE_OUT, cells, q).wait_recv()
        update_rows(q, theirs)

        @pl.when((q < depth) & (z == source_plane))
        def _():
            send_flux(1)

        @pl.when(q >= depth)
        def _():
            def block(i, carry):
                rows = pl.ds(pl.multiple_of(i * 16, 16), 16)
                out_ref[rows, z] = jnp.swapaxes(state[STEPS, 1 + z, :, rows, :], 0, 1)
                return carry

            lax.fori_loop(0, 16, block, 0)

    order = [
        (cross, LAG_CROSS),
        (pass_on, LAG_PASS),
        (finish_sums, LAG_FINISH),
        (third_sums, LAG_THIRD),
        (second_sums, LAG_SECOND),
        (first_sums, LAG_FIRST),
    ]

    def tick(t, carry):
        @pl.when(t == LAG_UPDATE)
        def _():
            finish_mix()

        for act, lag in order:

            @pl.when(t == lag)
            def _(act=act):
                act(extra, 0)

            @pl.when((t >= lag) & (t < lag + chunks))
            def _(act=act, lag=lag):
                act(cells, t - lag)

        @pl.when(t < 4)
        def _():
            for side in range(2):
                send_row(0, 2 * t + side)

        @pl.when((t >= LAG_UPDATE + 2) & (t < LAG_UPDATE + 6))
        def _():
            for side in range(2):
                send_row(1, 2 * (t - LAG_UPDATE - 2) + side)

        @pl.when(t == EDGE_TICK)
        def _():
            take_edge(0)

        @pl.when(t >= LAG_UPDATE)
        def _():
            update_rest(t - LAG_UPDATE)

        @pl.when((t >= LAG_CROSS) & (t < LAG_CROSS + chunks))
        def _():
            update_own(t - LAG_CROSS)

        @pl.when(t < chunks - AHEAD)
        def _():
            begin(t + AHEAD)
            message(CORE_SUM, cells, t + AHEAD).start()

        return carry

    def early(q, carry):
        begin(q)
        return carry

    lax.fori_loop(0, AHEAD, early, 0)
    pl.semaphore_wait(barrier, jnp.where(sends_halo, 5, 11))
    message(CORE_SUM, extra, 0).start()
    for q in range(AHEAD):
        message(CORE_SUM, cells, q).start()
    send_flux(0)
    lax.fori_loop(0, chunks + LAG_UPDATE, tick, 0)

    def drain(q, carry):
        for kind in range(9):
            message(kind, cells, q).wait_send()
        return carry

    lax.fori_loop(0, chunks, drain, 0)
    for kind in range(9):
        message(kind, extra, 0).wait_send()

    @pl.when(sends_halo)
    def _():
        for n in range(STEPS):
            for x in range(8):
                halo(n, x).wait_send()

    @pl.when(jnp.logical_not(sends_halo))
    def _():
        for n in range(STEPS):
            for k in range(8):
                flux(n, k, chip * 2 + core).wait_send()


def lane_shapes(chunks, piece):
    def vmem(lead, kind):
        return pltpu.VMEM((chunks,) + lead + piece, kind)

    return Lane(
        part=vmem((4,), F32),
        core_out=vmem((4,), BF16),
        core_in=vmem((4,), BF16),
        a_out=vmem((2,), BF16),
        a_in=vmem((2,), BF16),
        b_out=vmem((), BF16),
        b_in=vmem((), BF16),
        y_out=vmem((), BF16),
        y_in=vmem((), BF16),
        coeffs=vmem((8,), BF16),
        send=pltpu.SemaphoreType.DMA((9, chunks)),
        recv=pltpu.SemaphoreType.DMA((9, chunks)),
    )


def body(slabs, distribution, up_factor, down_factor, decay, wall_kind):
    local_vel, depth, width_x, width_y = distribution.shape
    rank = up_factor.shape[1]
    vmem = pl.BlockSpec(memory_space=pltpu.VMEM)
    anywhere = pl.BlockSpec(memory_space=pl.ANY)
    dma = pltpu.SemaphoreType.DMA
    return pl.pallas_call(
        functools.partial(kernel, depth, slabs),
        out_shape=pltpu.VMEM(distribution.shape, distribution.dtype),
        in_specs=[anywhere, vmem, vmem, vmem, vmem],
        out_specs=vmem,
        scratch_shapes=[
            pltpu.VMEM((STEPS + 1, depth + 2, width_x, local_vel, width_y), BF16),
            pltpu.VMEM((depth, local_vel, width_x, width_y), BF16),
            pltpu.VMEM((rank, local_vel), BF16),
            pltpu.VMEM((rank, rank), BF16),
            pltpu.VMEM((local_vel, width_y), F32),
            pltpu.VMEM((local_vel, width_y), F32),
            pltpu.VMEM((local_vel, width_y), F32),
            pltpu.VMEM((STEPS, width_x, width_y), F32),
            pltpu.VMEM((STEPS, 8, width_x, width_y), F32),
            dma((STEPS, 8)),
            dma((STEPS, 8)),
            dma((STEPS, 8)),
            dma((STEPS, 8)),
            dma((depth,)),
            *lane_shapes(STEPS * depth, (rank, width_y)),
            *lane_shapes(1, (rank // 4, width_y)),
        ],
        compiler_params=pltpu.CompilerParams(
            collective_id=0, has_side_effects=True, vmem_limit_bytes=VMEM_MIB * 2**20
        ),
        cost_estimate=pl.CostEstimate(
            flops=4 * STEPS * local_vel * rank * depth * width_x * width_y,
            bytes_accessed=4 * distribution.size,
            transcendentals=0,
        ),
        name="boltzmann_steps",
    )(distribution, up_factor, down_factor, decay.reshape(2, -1), wall_kind)


def solution(mesh):
    return jax.shard_map(
        functools.partial(body, mesh.shape["space"]),
        mesh=mesh,
        in_specs=(P("vel", "space", None, None), P("vel", None), P("vel", None), P("vel"), P()),
        out_specs=P("vel", "space", None, None),
        check_vma=False,
    )
```

```python
import functools
from typing import Any, NamedTuple

import jax
import jax.numpy as jnp
from jax import lax
from jax.experimental import pallas as pl
from jax.experimental.pallas import tpu as pltpu
from jax.sharding import PartitionSpec as P

NV = 16
STEPS = 2
MESH = pl.DeviceIdType.MESH
VMEM_MIB = 56

speed_range = 8.0
time_ratio = 0.08
wall_heat = 3.0

SPACING = speed_range / NV
MIDPOINT = (NV - 1) / 2.0
F32 = jnp.float32
BF16 = jnp.bfloat16

CORE_SUM, PASS_SUM, NEAR_SUM, LAST_SUM, PAIR_SUM, OUT_B, OUT_A, OUT_PASS, CORE_OUT = range(9)
LAG_FIRST, LAG_SECOND, LAG_THIRD, LAG_FINISH, LAG_PASS, LAG_CROSS, LAG_UPDATE = (
    0, 3, 7, 10, 13, 16, 17,
)
EDGE_TICK = 7
AHEAD = 3
MIX_TICK = 14


class Lane(NamedTuple):
    part: Any
    core_out: Any
    core_in: Any
    a_out: Any
    a_in: Any
    b_out: Any
    b_in: Any
    y_out: Any
    y_in: Any
    coeffs: Any
    send: Any
    recv: Any


def kernel(
    depth,
    slabs,
    dist_ref,
    up_ref,
    down_ref,
    decay_ref,
    wall_ref,
    out_ref,
    state,
    raw,
    down_t,
    mix,
    keep,
    slope_x,
    slope_y,
    flux_out,
    flux_in,
    halo_send,
    halo_recv,
    flux_send,
    flux_recv,
    in_sem,
    *lane_refs,
):
    count = len(Lane._fields)
    cells = Lane(*lane_refs[:count])
    extra = Lane(*lane_refs[count:])
    chunks = STEPS * depth
    slab = lax.axis_index("space")
    vel = lax.axis_index("vel")
    core = lax.rem(vel, 2)
    chip = lax.rem(vel // 2, 4)
    upper = vel // 8
    sign = 2 * upper - 1
    flip = chip + 1 - 2 * lax.rem(chip, 2)
    mirror = 3 - chip
    chip_a = flip * (1 - core) + mirror * core
    chip_b = mirror * (1 - core) + flip * core
    chip_o = lax.rem(chip + 2, 4)

    def device(pair, x, c):
        return (slab, pair * 8 + x * 2 + c)

    to_core = device(upper, chip, 1 - core)
    to_a = device(upper, chip_a, core)
    to_b = device(upper, chip_b, core)
    to_pair = device(1 - upper, chip, core)
    to_slab = (lax.rem(slab + sign + slabs, slabs), vel)
    last = depth - 1
    source_plane = last * upper
    target_plane = last * (1 - upper)
    halo_slot = (depth + 1) * (1 - upper)
    sends_halo = slab != (slabs - 1) * upper
    takes_halo = slab != (slabs - 1) * (1 - upper)
    mine = core * 4
    theirs = 4 - mine

    def level_of(q):
        return lax.rem(2 * depth - q + (depth - 2) * (q // depth), depth)

    def load(z):
        return pltpu.make_async_copy(dist_ref.at[:, z], raw.at[z], in_sem.at[z])

    def message(kind, lane, q):
        own = lane.coeffs.at[q, mine + chip]
        if kind == CORE_SUM:
            src, dst, target = lane.core_out.at[q], lane.core_in.at[q], to_core
        elif kind == PASS_SUM:
            src, dst, target = lane.a_out.at[q, 0], lane.a_in.at[q, 0], to_a
        elif kind == NEAR_SUM:
            src, dst, target = lane.a_out.at[q, 1], lane.a_in.at[q, 1], to_a
        elif kind == LAST_SUM:
            src, dst, target = lane.b_out.at[q], lane.b_in.at[q], to_b
        elif kind == PAIR_SUM:
            src, dst, target = lane.y_out.at[q], lane.y_in.at[q], to_pair
        elif kind == OUT_B:
            src, dst, target = own, own, to_b
        elif kind == OUT_A:
            src, dst, target = own, own, to_a
        elif kind == OUT_PASS:
            src = lane.coeffs.at[q, mine + chip_b]
            dst, target = src, to_a
        else:
            src = lane.coeffs.at[q, pl.ds(mine, 4)]
            dst, target = src, to_core
        return pltpu.make_async_remote_copy(
            src_ref=src,
            dst_ref=dst,
            send_sem=lane.send.at[kind, q],
            recv_sem=lane.recv.at[kind, q],
            device_id=target,
            device_id_type=MESH,
        )

    def halo(n, x):
        return pltpu.make_async_remote_copy(
            src_ref=state.at[n, 1 + source_plane, x],
            dst_ref=state.at[n, halo_slot, x],
            send_sem=halo_send.at[n, x],
            recv_sem=halo_recv.at[n, x],
            device_id=to_slab,
            device_id_type=MESH,
        )

    def flux(n, k, sender):
        return pltpu.make_async_remote_copy(
            src_ref=flux_out.at[n],
            dst_ref=flux_in.at[n, sender],
            send_sem=flux_send.at[n, k],
            recv_sem=flux_recv.at[n, sender],
            device_id=(slab, (1 - upper) * 8 + k),
            device_id_type=MESH,
        )

    barrier = pltpu.get_barrier_semaphore()

    def greet(target):
        pl.semaphore_signal(barrier, inc=1, device_id=target, device_id_type=MESH)

    for target in (to_core, to_a, to_b, to_pair):
        greet(target)

    @pl.when(takes_halo)
    def _():
        greet((slab - sign, vel))

    @pl.when(jnp.logical_not(takes_halo))
    def _():
        for k in range(1, 8):
            greet((slab, (1 - upper) * 8 + lax.rem(chip * 2 + core + k, 8)))

    for q in range(depth):
        load((depth - q) % depth).start()

    down_t[...] = down_ref[...].T
    for j in range(4):
        for base, left in ((theirs, True), (mine, False)):
            rows = pl.ds(pl.multiple_of((base + j) * 32, 32), 32)
            both = jnp.dot(down_t[rows, :], up_ref[...], preferred_element_type=F32)
            for side in range(2):
                value = both[:, 128 * side : 128 * side + 128]
                if left:
                    extra.core_out[0, j, 32 * side : 32 * side + 32] = value.astype(BF16)
                else:
                    extra.part[0, j, 32 * side : 32 * side + 32] = value
    ids = lax.broadcasted_iota(jnp.int32, (256, 128), 0)
    speed_x = jnp.abs(((ids >> 4).astype(F32) - MIDPOINT) * SPACING)
    speed_y = jnp.abs(((ids & 15).astype(F32) - MIDPOINT) * SPACING)
    speed_z = jnp.abs((vel.astype(F32) - MIDPOINT) * SPACING)
    decay = jnp.concatenate(
        [jnp.broadcast_to(decay_ref[i : i + 1, :], (128, 128)).T for i in range(2)], axis=0
    )
    keep[...] = 1.0 - time_ratio * (speed_x + speed_y + speed_z + decay)
    slope_x[...] = time_ratio * speed_x
    slope_y[...] = time_ratio * speed_y
    slope_z = time_ratio * speed_z

    def arrange(q, carry):
        z = level_of(q)
        load(z).wait()

        def block(i, inner):
            rows = pl.ds(pl.multiple_of(i * 16, 16), 16)
            state[0, 1 + z, :, rows, :] = jnp.swapaxes(raw[z, rows], 0, 1)
            return inner

        return lax.fori_loop(0, 16, block, carry)

    lax.fori_loop(0, depth, arrange, 0)

    def send_row(n, x):
        @pl.when(sends_halo)
        def _():
            halo(n, x).start()

    def send_flux(n):
        @pl.when(jnp.logical_not(sends_halo))
        def _():
            for x in range(8):
                plane = state[n, 1 + source_plane, x].astype(F32)
                flux_out[n, x : x + 1, :] = speed_z * jnp.sum(plane, axis=0, keepdims=True)
            for k in range(8):
                flux(n, k, chip * 2 + core).start()

    def take_edge(n):
        @pl.when(takes_halo)
        def _():
            for x in range(8):
                halo(n, x).wait_recv()

        @pl.when(jnp.logical_not(takes_halo))
        def _():
            wall(n)

    def wall(n):
        for k in range(8):
            flux(n, k, k).wait_recv()
        line = (lax.broadcasted_iota(jnp.int32, (8, 128), 1).astype(F32) - MIDPOINT) * SPACING
        valid = lax.broadcasted_iota(jnp.int32, (8, 128), 1) < NV
        gauss = jnp.where(valid, jnp.exp(-0.5 * line * line), 0.0)
        flow = jnp.sum(jnp.maximum(line, 0.0) * gauss, axis=1, keepdims=True)
        mass = jnp.sum(gauss, axis=1, keepdims=True)
        norm = flow * mass * mass
        out = flux_in[n, 0]
        for k in range(1, 8):
            out = out + flux_in[n, k]
        kind = wall_ref[1 - upper]
        opened = jnp.where(kind == 2, 0.0, 1.0)
        sigma = out / norm * opened
        heating = jnp.where(kind == 1, wall_heat, 0.0)
        rows = lax.broadcasted_iota(jnp.int32, (256, 128), 0)
        one_x = ((rows >> 4).astype(F32) - MIDPOINT) * SPACING
        one_y = ((rows & 15).astype(F32) - MIDPOINT) * SPACING
        half_sq = 0.5 * (one_x * one_x + one_y * one_y + speed_z * speed_z)
        maxwell = jnp.exp(-half_sq)
        energy = half_sq - 1.5
        for x in range(8):
            ghost = maxwell * (sigma[x : x + 1] + heating[x : x + 1] * energy)
            state[n, halo_slot, x] = ghost.astype(BF16)

    def drift(n, z, x, half):
        rows = slice(128 * half, 128 * half + 128)
        beside = lax.rem(x + (1 if half == 0 else 7), 8)
        centre = state[n, 1 + z, x, rows].astype(F32)
        wind_z = state[n, 1 + z - sign, x, rows].astype(F32)
        wind_x = state[n, 1 + z, beside, rows].astype(F32)
        split = centre.reshape(8, 16, 128)
        wind_y = jnp.concatenate(
            [pltpu.roll(split[:, :8], 127, 2), pltpu.roll(split[:, 8:], 1, 2)], axis=1
        ).reshape(128, 128)
        return (
            keep[rows] * centre
            + slope_z * wind_z
            + slope_x[rows] * wind_x
            + slope_y[rows] * wind_y
        )

    def begin(q):
        n, z = q // depth, level_of(q)

        @pl.when(q >= depth)
        def _():
            def row(x, carry):
                for half in range(2):
                    rows = slice(128 * half, 128 * half + 128)
                    state[STEPS, 1 + z, x, rows] = drift(0, z, x, half).astype(BF16)
                return carry

            lax.fori_loop(0, 8, row, 0)

        def project(x):
            pair = jnp.concatenate(
                [state[STEPS * n, 1 + z, x], state[STEPS * n, 1 + z, x + 1]], axis=1
            )
            return jnp.dot(down_t[...], pair, preferred_element_type=F32)

        for j in range(2):
            both = project(theirs + 2 * j)
            cells.core_out[q, 2 * j] = both[:, :128].astype(BF16)
            cells.core_out[q, 2 * j + 1] = both[:, 128:].astype(BF16)
        for j in range(2):
            both = project(mine + 2 * j)
            cells.part[q, 2 * j] = both[:, :128]
            cells.part[q, 2 * j + 1] = both[:, 128:]

    def chip_sum(lane, q, j):
        return lane.part[q, j] + lane.core_in[q, j].astype(F32)

    def first_sums(lane, q):
        message(CORE_SUM, lane, q).wait_recv()
        lane.a_out[q, 0] = chip_sum(lane, q, chip_o).astype(BF16)
        message(PASS_SUM, lane, q).start()
        lane.a_out[q, 1] = chip_sum(lane, q, chip_a).astype(BF16)
        message(NEAR_SUM, lane, q).start()

    def second_sums(lane, q):
        message(PASS_SUM, lane, q).wait_recv()
        total = chip_sum(lane, q, chip_b) + lane.a_in[q, 0].astype(F32)
        lane.b_out[q] = total.astype(BF16)
        message(LAST_SUM, lane, q).start()

    def third_sums(lane, q):
        message(NEAR_SUM, lane, q).wait_recv()
        message(LAST_SUM, lane, q).wait_recv()
        total = chip_sum(lane, q, chip) + lane.a_in[q, 1].astype(F32)
        total = total + lane.b_in[q].astype(F32)
        lane.part[q, chip] = total
        lane.y_out[q] = total.astype(BF16)
        message(PAIR_SUM, lane, q).start()

    def finish_sums(lane, q):
        message(PAIR_SUM, lane, q).wait_recv()
        if lane is cells:

            @pl.when(q >= depth)
            def _():
                before = lax.rem(depth - level_of(q), depth)
                known = lane.coeffs[before, mine + chip]
                gain = jnp.dot(mix[...], known, preferred_element_type=F32)
                lane.part[q, chip] += time_ratio * gain

        total = lane.part[q, chip] + lane.y_in[q].astype(F32)
        lane.coeffs[q, mine + chip] = total.astype(BF16)
        message(OUT_B, lane, q).start()
        message(OUT_A, lane, q).start()

    def pass_on(lane, q):
        message(OUT_B, lane, q).wait_recv()
        message(OUT_PASS, lane, q).start()

    def cross(lane, q):
        message(OUT_A, lane, q).wait_recv()
        message(OUT_PASS, lane, q).wait_recv()
        message(CORE_OUT, lane, q).start()

    def finish_mix():
        message(CORE_OUT, extra, 0).wait_recv()
        for j in range(8):
            for side in range(2):
                piece = extra.coeffs[0, j, 32 * side : 32 * side + 32]
                mix[32 * j : 32 * j + 32, 128 * side : 128 * side + 128] = piece

    def update_rows(q, base):
        n, z = q // depth, level_of(q)

        def row_pair(i, carry):
            first = base + 2 * i
            pair = jnp.concatenate([cells.coeffs[q, first], cells.coeffs[q, first + 1]], axis=1)
            gained = jnp.dot(up_ref[...], pair, preferred_element_type=F32)
            for side in range(2):
                x = first + side
                for half in range(2):
                    rows = slice(128 * half, 128 * half + 128)
                    new = (
                        drift(n, z, x, half)
                        + time_ratio * gained[rows, 128 * side : 128 * side + 128]
                    )
                    state[n + 1, 1 + z, x, rows] = new.astype(BF16)
            return carry

        lax.fori_loop(0, 2, row_pair, 0)

    def update_own(q):
        @pl.when((q >= depth) & (level_of(q) == target_plane))
        def _():
            take_edge(1)

        update_rows(q, mine)

    def update_rest(q):
        z = level_of(q)
        message(CORE_OUT, cells, q).wait_recv()
        update_rows(q, theirs)

        @pl.when((q < depth) & (z == source_plane))
        def _():
            send_flux(1)

        @pl.when(q >= depth)
        def _():
            def block(i, carry):
                rows = pl.ds(pl.multiple_of(i * 16, 16), 16)
                out_ref[rows, z] = jnp.swapaxes(state[STEPS, 1 + z, :, rows, :], 0, 1)
                return carry

            lax.fori_loop(0, 16, block, 0)

    order = [
        (pass_on, LAG_PASS, 10),
        (second_sums, LAG_SECOND, 3),
        (first_sums, LAG_FIRST, 0),
        (finish_sums, LAG_FINISH, 8),
        (third_sums, LAG_THIRD, 6),
        (cross, LAG_CROSS, 12),
    ]

    def tick(t, carry):
        @pl.when(t == MIX_TICK)
        def _():
            finish_mix()

        for act, lag, once in order:

            @pl.when(t == once)
            def _(act=act):
                act(extra, 0)

            @pl.when((t >= lag) & (t < lag + chunks))
            def _(act=act, lag=lag):
                act(cells, t - lag)

        @pl.when(t < 4)
        def _():
            for side in range(2):
                send_row(0, 2 * t + side)

        @pl.when((t >= LAG_UPDATE + 2) & (t < LAG_UPDATE + 6))
        def _():
            for side in range(2):
                send_row(1, 2 * (t - LAG_UPDATE - 2) + side)

        @pl.when(t == EDGE_TICK)
        def _():
            take_edge(0)

        @pl.when(t >= LAG_UPDATE)
        def _():
            update_rest(t - LAG_UPDATE)

        @pl.when((t >= LAG_CROSS) & (t < LAG_CROSS + chunks))
        def _():
            update_own(t - LAG_CROSS)

        @pl.when(t < chunks - AHEAD)
        def _():
            begin(t + AHEAD)
            message(CORE_SUM, cells, t + AHEAD).start()

        return carry

    def early(q, carry):
        begin(q)
        return carry

    lax.fori_loop(0, AHEAD, early, 0)
    pl.semaphore_wait(barrier, jnp.where(sends_halo, 5, 11))
    message(CORE_SUM, extra, 0).start()
    for q in range(AHEAD):
        message(CORE_SUM, cells, q).start()
    send_flux(0)
    lax.fori_loop(0, chunks + LAG_UPDATE, tick, 0)

    def drain(q, carry):
        for kind in range(9):
            message(kind, cells, q).wait_send()
        return carry

    lax.fori_loop(0, chunks, drain, 0)
    for kind in range(9):
        message(kind, extra, 0).wait_send()

    @pl.when(sends_halo)
    def _():
        for n in range(STEPS):
            for x in range(8):
                halo(n, x).wait_send()

    @pl.when(jnp.logical_not(sends_halo))
    def _():
        for n in range(STEPS):
            for k in range(8):
                flux(n, k, chip * 2 + core).wait_send()


def lane_shapes(chunks, piece):
    def vmem(lead, kind):
        return pltpu.VMEM((chunks,) + lead + piece, kind)

    return Lane(
        part=vmem((4,), F32),
        core_out=vmem((4,), BF16),
        core_in=vmem((4,), BF16),
        a_out=vmem((2,), BF16),
        a_in=vmem((2,), BF16),
        b_out=vmem((), BF16),
        b_in=vmem((), BF16),
        y_out=vmem((), BF16),
        y_in=vmem((), BF16),
        coeffs=vmem((8,), BF16),
        send=pltpu.SemaphoreType.DMA((9, chunks)),
        recv=pltpu.SemaphoreType.DMA((9, chunks)),
    )


def body(slabs, distribution, up_factor, down_factor, decay, wall_kind):
    local_vel, depth, width_x, width_y = distribution.shape
    rank = up_factor.shape[1]
    vmem = pl.BlockSpec(memory_space=pltpu.VMEM)
    anywhere = pl.BlockSpec(memory_space=pl.ANY)
    dma = pltpu.SemaphoreType.DMA
    return pl.pallas_call(
        functools.partial(kernel, depth, slabs),
        out_shape=pltpu.VMEM(distribution.shape, distribution.dtype),
        in_specs=[anywhere, vmem, vmem, vmem, vmem],
        out_specs=vmem,
        scratch_shapes=[
            pltpu.VMEM((STEPS + 1, depth + 2, width_x, local_vel, width_y), BF16),
            pltpu.VMEM((depth, local_vel, width_x, width_y), BF16),
            pltpu.VMEM((rank, local_vel), BF16),
            pltpu.VMEM((rank, rank), BF16),
            pltpu.VMEM((local_vel, width_y), F32),
            pltpu.VMEM((local_vel, width_y), F32),
            pltpu.VMEM((local_vel, width_y), F32),
            pltpu.VMEM((STEPS, width_x, width_y), F32),
            pltpu.VMEM((STEPS, 8, width_x, width_y), F32),
            dma((STEPS, 8)),
            dma((STEPS, 8)),
            dma((STEPS, 8)),
            dma((STEPS, 8)),
            dma((depth,)),
            *lane_shapes(STEPS * depth, (rank, width_y)),
            *lane_shapes(1, (rank // 4, width_y)),
        ],
        compiler_params=pltpu.CompilerParams(
            collective_id=0, has_side_effects=True, vmem_limit_bytes=VMEM_MIB * 2**20
        ),
        cost_estimate=pl.CostEstimate(
            flops=4 * STEPS * local_vel * rank * depth * width_x * width_y,
            bytes_accessed=4 * distribution.size,
            transcendentals=0,
        ),
        name="boltzmann_steps",
    )(distribution, up_factor, down_factor, decay.reshape(2, -1), wall_kind)


def solution(mesh):
    return jax.shard_map(
        functools.partial(body, mesh.shape["space"]),
        mesh=mesh,
        in_specs=(P("vel", "space", None, None), P("vel", None), P("vel", None), P("vel"), P()),
        out_specs=P("vel", "space", None, None),
        check_vma=False,
    )
```
